32 devices in a mesh: sta: 8 (over z, y), day: 4 (over x, core).
Axes of the slice: x: 2, y: 2, z: 4, core: 2. Of those that a mesh axis runs over, the one named last changes fastest.
Arguments:
- solution: float32 [4, 4096, 4096], P(None, 'sta', 'day'), may hold values from -6 to 6
- residual: float32 [4, 4096, 4096], P(None, 'sta', 'day'), may hold values from -6 to 6
- direction: float32 [4, 4096, 4096], P(None, 'sta', 'day'), may hold values from -6 to 6
- observed: int32 [4096, 4096], P('sta', 'day'), may hold values 0 or 1
- coords: float32 [2, 4096], replicated, may hold values from 0 to 1
- day_features: float32 [4, 4096], replicated, may hold values from 0 to 1
- noise: float32 [4096], P('sta'), may hold values from 0.1 to 1
Outputs:
- new_solution: float32 [4, 4096, 4096], P(None, 'sta', 'day')
- new_residual: float32 [4, 4096, 4096], P(None, 'sta', 'day')
- new_direction: float32 [4, 4096, 4096], P(None, 'sta', 'day')
The draws below stay inside these ranges and needn't reach their ends.
All inputs are finite; a program needn't handle non-finite values. No bound on the sum of `observed` on one device may be relied on, other than what follows from the above.
Results may differ from the reference program's by a relative error of at most 0.000054.
Values sent between devices are 32-bit elements; how exact they have to be, the bound alone decides.
No kernel may reach another device: no remote copies, remote signals or barrier semaphores. Data moves between devices by JAX's collectives and lax.ppermute only.
A program may use at most 192 MiB of HBM per device.

```python
import math
import jax
import jax.numpy as jnp
from jax import lax

STATIONS = 4096
DAYS = 4096
PROBES = 4
FEAT = 4


def draw_direction(key, part):
    key = jax.random.fold_in(key, 11)
    key_white = jax.random.fold_in(key, 1)
    key_modes = jax.random.fold_in(key, 2)
    key_phase = jax.random.fold_in(key, 3)
    key_station = jax.random.fold_in(key, 4)
    white = jax.random.normal(key_white, (PROBES, STATIONS, DAYS), jnp.float32)
    amplitude = 0.6
    lowest = DAYS * 22 // 100
    highest = DAYS * 97 // 100
    band = (highest - lowest) // 4
    offsets = jax.random.randint(key_modes, (PROBES, 4), 0, band, jnp.int32)
    modes = lowest + band * jnp.arange(4, dtype=jnp.int32)[None, :] + offsets
    phases = jax.random.uniform(key_phase, (PROBES, 4, 1), jnp.float32, 0.0, 2.0 * math.pi)
    days = jnp.arange(DAYS, dtype=jnp.int32)
    turns = modes[:, :, None] * (2 * days + 1)[None, None, :] % (4 * DAYS)
    angles = turns.astype(jnp.float32) * (math.pi / (2.0 * DAYS)) + phases
    wave = amplitude * jnp.sum(jnp.cos(angles), axis=1)
    station_field = jax.random.uniform(key_station, (PROBES, STATIONS, 1), jnp.float32, 0.5, 1.5)
    return jnp.clip(white + station_field * wave[:, None, :], -6.0, 6.0)


def plant(entries, rng, smallest, largest):
    place = [jax.random.randint(jax.random.fold_in(rng, axis), (), 0, length) for axis, length in enumerate(entries.shape)]
    main_axis = entries.shape.index(max(entries.shape))
    neighbour = place[:main_axis] + [(place[main_axis] + 1) % entries.shape[main_axis]] + place[main_axis + 1:]
    return entries.at[tuple(place)].set(smallest).at[tuple(neighbour)].set(largest)


def block_levels(stream_key, dims, cuts, smallest, largest):
    def one(dim, shards_of):
        heights = jax.random.uniform(jax.random.fold_in(jax.random.fold_in(stream_key, 6), dim), (shards_of,), jnp.float32, smallest / len(cuts), largest / len(cuts))
        return jnp.repeat(jnp.exp(heights), dims[dim] // shards_of).reshape((-1,) + (1,) * (len(dims) - dim - 1))

    loudness = one(*cuts[0])
    for cut in cuts[1:]:
        loudness = loudness * one(*cut)
    return loudness


def scatter_about(key, dims, spread, reach, cuts=(), kind=jnp.bfloat16):
    loudness = block_levels(key, dims, cuts, -0.22, 0.18) if cuts else 1.0
    values = jax.random.normal(key, dims, jnp.float32) * spread * loudness
    return jnp.minimum(jnp.maximum(values, -reach), reach).astype(kind)


def setup_inputs(seed: int = 0) -> dict:
    seeds = jax.random.split(jax.random.key(seed), 8)
    solution = scatter_about(seeds[0], (PROBES, STATIONS, DAYS), 1.0, 6.0, ((1, 8), (2, 4)), jnp.float32)
    residual = scatter_about(seeds[1], (PROBES, STATIONS, DAYS), 1.0, 6.0, ((1, 8), (2, 4)), jnp.float32)
    direction = draw_direction(jax.random.fold_in(seeds[7], 71), 0)
    observed = plant((jax.random.randint(seeds[3], (STATIONS, DAYS), 0, 4) < 3).astype(jnp.int32), jax.random.fold_in(seeds[3], 1), 0, 1)
    coords = jnp.clip(jax.random.uniform(seeds[4], (2, STATIONS), jnp.float32, 0.0, 1.0), 0.0, 1.0)
    day_features = jnp.clip(jax.random.uniform(seeds[5], (FEAT, DAYS), jnp.float32, 0.0, 1.0), 0.0, 1.0)
    noise = jnp.clip(jnp.exp(math.log(1.0) - 2.3025851 * jax.random.uniform(seeds[6], (STATIONS,), jnp.float32) ** block_levels(seeds[6], (STATIONS,), ((0, 8),), -0.2, 0.2)), 0.1, 1.0)
    return dict(solution=solution, residual=residual, direction=direction, observed=observed, coords=coords, day_features=day_features, noise=noise)


space_range = 0.5
time_range = 0.5

def space_kernel(coords):
    dx = coords[0][:, None] - coords[0][None, :]
    dy = coords[1][:, None] - coords[1][None, :]
    dist = jnp.sqrt(dx * dx + dy * dy)
    return jnp.exp(-dist / space_range) * (2.0 / STATIONS ** 0.5)

def time_kernel(day_features):
    total = jnp.zeros((DAYS, DAYS), jnp.float32)
    for feature in range(FEAT):
        diff = day_features[feature][:, None] - day_features[feature][None, :]
        total = total + diff * diff
    return jnp.exp(-jnp.sqrt(total) / time_range) * (2.0 / DAYS ** 0.5)

def reference(solution, residual, direction, observed, coords, day_features, noise):
    weight = observed.astype(jnp.float32)
    masked = weight[None] * direction
    inner = jnp.einsum('pst,tu->psu', masked, time_kernel(day_features), precision=lax.Precision.HIGHEST)
    outer = jnp.einsum('ik,pku->piu', space_kernel(coords), inner, precision=lax.Precision.HIGHEST)
    image = weight[None] * outer + noise[None, :, None] * direction
    norm_now = lax.optimization_barrier(jnp.sum(residual * residual, axis=(1, 2)))
    curve = lax.optimization_barrier(jnp.sum(direction * image, axis=(1, 2)))
    alpha = (norm_now / curve)[:, None, None]
    new_solution = solution + alpha * direction
    new_residual = residual - alpha * image
    norm_next = lax.optimization_barrier(jnp.sum(new_residual * new_residual, axis=(1, 2)))
    beta = (norm_next / norm_now)[:, None, None]
    new_direction = new_residual + beta * direction
    return (new_solution, new_residual, new_direction)
```

```python
import functools
import math

import jax
import jax.numpy as jnp
from jax import lax
from jax.experimental import pallas as pl
from jax.experimental.pallas import tpu as pltpu
from jax.sharding import PartitionSpec as P

STATIONS = 4096
DAYS = 4096
FEAT = 4

space_range = 0.5
time_range = 0.5

MIB = 1 << 20


def params(limit):
    return pltpu.CompilerParams(vmem_limit_bytes=limit * MIB)


def mask_kernel(observed, direction, out):
    out[0] = observed[...].astype(jnp.float32) * direction[0]


def mask_call(observed, direction, probe, parts):
    _, s_loc, t_loc = direction.shape
    width = t_loc // parts
    return pl.pallas_call(
        mask_kernel,
        grid=(parts,),
        in_specs=[
            pl.BlockSpec((s_loc, width), lambda j: (0, j)),
            pl.BlockSpec((1, s_loc, width), lambda j: (probe, 0, j)),
        ],
        out_specs=pl.BlockSpec((1, s_loc, width), lambda j: (j, 0, 0)),
        out_shape=jax.ShapeDtypeStruct((parts, s_loc, width), jnp.float32),
        compiler_params=params(24),
        cost_estimate=pl.CostEstimate(flops=s_loc * t_loc, bytes_accessed=12 * s_loc * t_loc, transcendentals=0),
        name="mask",
    )(observed, direction)


def entries_kernel(features, slope, shift, rows_order, cols_order, rows, cols, high, low):
    step = 32

    @pl.loop(0, rows.shape[0] // step)
    def _(index):
        at = pl.ds(pl.multiple_of(index * step, step), step)
        mine = rows[at, :]
        total = None
        for feature in range(features):
            diff = mine[:, feature : feature + 1] - cols[feature : feature + 1, :]
            total = diff * diff if total is None else total + diff * diff
        dist = total * lax.rsqrt(jnp.maximum(total, 1e-37))
        value = jnp.exp2(dist * slope + shift)
        top = value.astype(jnp.bfloat16)
        high[at, :] = top
        low[at, :] = (value - top.astype(jnp.float32)).astype(jnp.bfloat16)


def entries_call(table, rows_order, cols_order, tile, reach, order, name):
    features = table.shape[0]
    n_rows, n_cols = rows_order.shape[0], cols_order.shape[0]
    shape = (n_rows * tile, n_cols * tile)
    count = shape[0] * shape[1]
    out_spec = pl.BlockSpec((tile, tile), lambda i, j, ro, co: (i, j))
    slope = -1.0 / (reach * math.log(2.0))
    shift = math.log2(2.0 / order**0.5)
    return pl.pallas_call(
        functools.partial(entries_kernel, features, slope, shift),
        grid_spec=pltpu.PrefetchScalarGridSpec(
            num_scalar_prefetch=2,
            grid=(n_rows, n_cols),
            in_specs=[
                pl.BlockSpec((tile, features), lambda i, j, ro, co: (ro[i], 0)),
                pl.BlockSpec((features, tile), lambda i, j, ro, co: (0, co[j])),
            ],
            out_specs=[out_spec, out_spec],
        ),
        out_shape=[jax.ShapeDtypeStruct(shape, jnp.bfloat16)] * 2,
        compiler_params=params(24),
        cost_estimate=pl.CostEstimate(flops=16 * count, bytes_accessed=4 * count, transcendentals=2 * count),
        name=name,
    )(rows_order, cols_order, table.T, table)


def split(value):
    top = value.astype(jnp.bfloat16)
    return top, (value - top.astype(jnp.float32)).astype(jnp.bfloat16)


def dot(a, b):
    return jnp.dot(a, b, preferred_element_type=jnp.float32)


def space_kernel(count, *refs):
    cells = refs[:count]
    high, low, out, cells_high, cells_low = refs[count:]
    blocks, s_loc, _ = cells[0].shape

    @pl.when(pl.program_id(0) == 0)
    def _():
        for k in range(count):
            for b in range(blocks):
                at = pl.ds((k * blocks + b) * s_loc, s_loc)
                cells_high[at, :], cells_low[at, :] = split(cells[k][b])

    total = dot(high[...], cells_high[...])
    total += dot(high[...], cells_low[...])
    total += dot(low[...], cells_high[...])
    out[0] = total


def space_call(cells, high, low):
    blocks, s_loc, width = cells[0].shape
    stations = high.shape[1]
    whole = pl.BlockSpec((blocks, s_loc, width), lambda i: (0, 0, 0))
    matrix = pl.BlockSpec((s_loc, stations), lambda i: (i, 0))
    return pl.pallas_call(
        functools.partial(space_kernel, len(cells)),
        grid=(blocks,),
        in_specs=[whole] * len(cells) + [matrix, matrix],
        out_specs=pl.BlockSpec((1, s_loc, width), lambda i: (i, 0, 0)),
        out_shape=jax.ShapeDtypeStruct((blocks, s_loc, width), jnp.float32),
        scratch_shapes=[pltpu.VMEM((stations, width), jnp.bfloat16)] * 2,
        compiler_params=params(48),
        cost_estimate=pl.CostEstimate(
            flops=6 * blocks * s_loc * stations * width,
            bytes_accessed=4 * blocks * s_loc * stations + 8 * stations * width,
            transcendentals=0,
        ),
        name="space",
    )(*cells, high, low)


def time_kernel(count, *refs):
    cells = refs[:count]
    high, low, out, cells_high, cells_low = refs[count:]
    blocks, _, width = cells[0].shape

    @pl.when(pl.program_id(0) == 0)
    def _():
        for k in range(count):
            for b in range(blocks):
                at = pl.ds((k * blocks + b) * width, width)
                cells_high[:, at], cells_low[:, at] = split(cells[k][b])

    total = dot(cells_high[...], high[...])
    total += dot(cells_low[...], high[...])
    total += dot(cells_high[...], low[...])
    out[0] = total


def time_call(cells, high, low):
    blocks, s_loc, width = cells[0].shape
    days = high.shape[0]
    whole = pl.BlockSpec((blocks, s_loc, width), lambda i: (0, 0, 0))
    matrix = pl.BlockSpec((days, width), lambda i: (0, i))
    return pl.pallas_call(
        functools.partial(time_kernel, len(cells)),
        grid=(blocks,),
        in_specs=[whole] * len(cells) + [matrix, matrix],
        out_specs=pl.BlockSpec((1, s_loc, width), lambda i: (i, 0, 0)),
        out_shape=jax.ShapeDtypeStruct((blocks, s_loc, width), jnp.float32),
        scratch_shapes=[pltpu.VMEM((s_loc, days), jnp.bfloat16)] * 2,
        compiler_params=params(48),
        cost_estimate=pl.CostEstimate(
            flops=6 * blocks * s_loc * days * width,
            bytes_accessed=4 * blocks * width * days + 8 * days * s_loc,
            transcendentals=0,
        ),
        name="time",
    )(*cells, high, low)


def sums_kernel(observed, noise, residual, direction, outer, out, total):
    step = pl.program_id(0)

    @pl.when(step == 0)
    def _():
        total[...] = jnp.zeros_like(total)

    res = residual[0]
    way = direction[0]
    image = observed[...].astype(jnp.float32) * outer[0] + noise[...] * way
    for row, product in enumerate((res * res, way * image, res * image, image * image)):
        total[row : row + 1, :] += jnp.sum(product, axis=0, keepdims=True)

    @pl.when(step == pl.num_programs(0) - 1)
    def _():
        out[...] = jnp.broadcast_to(jnp.sum(total[...], axis=1, keepdims=True), out.shape)


def sums_call(observed, noise, residual, direction, outer, probe):
    parts, s_loc, width = outer.shape
    column = pl.BlockSpec((1, s_loc, width), lambda j: (probe, 0, j))
    return pl.pallas_call(
        sums_kernel,
        grid=(parts,),
        in_specs=[
            pl.BlockSpec((s_loc, width), lambda j: (0, j)),
            pl.BlockSpec((s_loc, 1), lambda j: (0, 0)),
            column,
            column,
            pl.BlockSpec((1, s_loc, width), lambda j: (j, 0, 0)),
        ],
        out_specs=pl.BlockSpec((8, 128), lambda j: (0, 0)),
        out_shape=jax.ShapeDtypeStruct((8, 128), jnp.float32),
        scratch_shapes=[pltpu.VMEM((8, width), jnp.float32)],
        compiler_params=params(32),
        cost_estimate=pl.CostEstimate(
            flops=12 * parts * s_loc * width, bytes_accessed=16 * parts * s_loc * width, transcendentals=0
        ),
        name="sums",
    )(observed, noise, residual, direction, outer)


def update_kernel(row, parts, observed, noise, solution, residual, direction, outer, *refs):
    new_solution, new_residual, new_direction = refs[-3:]
    totals = jnp.sum(parts[:, row * 8 : row * 8 + 8, :], axis=0)
    rr, pap, cross, square = (totals[k : k + 1, :1] for k in range(4))
    alpha = rr / pap
    rr_next = rr + alpha * (alpha * square - 2.0 * cross)
    beta = rr_next / rr
    way = direction[0]
    image = observed[...].astype(jnp.float32) * outer[0] + noise[...] * way
    fresh = residual[0] - alpha * image
    new_solution[0] = solution[0] + alpha * way
    new_residual[0] = fresh
    new_direction[0] = fresh + beta * way


def update_call(stats, row, observed, noise, solution, residual, direction, outer, probe, earlier):
    parts, s_loc, width = outer.shape
    column = pl.BlockSpec((1, s_loc, width), lambda j: (probe, 0, j))
    shape = jax.ShapeDtypeStruct(direction.shape, jnp.float32)
    return pl.pallas_call(
        functools.partial(update_kernel, row),
        grid=(parts,),
        in_specs=[
            pl.BlockSpec(stats.shape, lambda j: (0, 0, 0)),
            pl.BlockSpec((s_loc, width), lambda j: (0, j)),
            pl.BlockSpec((s_loc, 1), lambda j: (0, 0)),
            column,
            column,
            column,
            pl.BlockSpec((1, s_loc, width), lambda j: (j, 0, 0)),
        ]
        + [pl.BlockSpec(memory_space=pl.ANY)] * len(earlier),
        out_specs=[column] * 3,
        out_shape=[shape] * 3,
        input_output_aliases={7 + k: k for k in range(len(earlier))},
        compiler_params=params(40),
        cost_estimate=pl.CostEstimate(
            flops=12 * parts * s_loc * width, bytes_accessed=32 * parts * s_loc * width, transcendentals=0
        ),
        name="update",
    )(stats, observed, noise, solution, residual, direction, outer, *earlier)


def shards(solution, residual, direction, observed, coords, day_features, noise):
    n_sta = lax.axis_size("sta")
    n_day = lax.axis_size("day")
    probes, s_loc, t_loc = direction.shape
    n_z = math.gcd(n_sta, 4)
    n_y = n_sta // n_z
    n_core = math.gcd(n_day, 2)
    n_x = n_day // n_core
    sta = lax.axis_index("sta")
    day = lax.axis_index("day")
    z_groups = [[z * n_y + y for z in range(n_z)] for y in range(n_y)]

    def over_z(pieces):
        return lax.all_to_all(pieces, "sta", 0, 0, axis_index_groups=z_groups, tiled=True)

    def over_y(cells):
        found = [cells]
        for k in range(1, n_y):
            pairs = [(z * n_y + y, z * n_y + (y + k) % n_y) for z in range(n_z) for y in range(n_y)]
            found.append(lax.ppermute(cells, "sta", pairs))
        return found

    def over_day(cells):
        found = []
        swap = [(j, j - j % n_core + (j + 1) % n_core) for j in range(n_day)]
        for k in range(n_x):
            pairs = [(x * n_core + c, (x + k) % n_x * n_core + c) for x in range(n_x) for c in range(n_core)]
            here = lax.ppermute(cells, "day", pairs) if k else cells
            found.append(here)
            if n_core > 1:
                found.append(lax.ppermute(here, "day", swap))
        return found

    def over_all(block):
        many = jnp.broadcast_to(block[None], (n_sta * n_day, *block.shape))
        return lax.all_to_all(many, ("sta", "day"), 0, 0, tiled=True)

    tile_s = math.gcd(512, s_loc)
    tile_t = math.gcd(512, t_loc)

    def tiles(blocks, size, tile):
        each = size // tile
        return (blocks[:, None] * each + jnp.arange(each, dtype=jnp.int32)[None, :]).reshape(-1)

    z_index = jnp.arange(n_z, dtype=jnp.int32)
    y_index = jnp.arange(n_y, dtype=jnp.int32)
    y_here = sta % n_y
    mine_s = z_index * n_y + y_here
    all_s = (z_index[None, :] * n_y + (y_here - y_index[:, None]) % n_y).reshape(-1)
    x_index = jnp.arange(n_x, dtype=jnp.int32)
    c_index = jnp.arange(n_core, dtype=jnp.int32)
    x_here, c_here = day // n_core, day % n_core
    all_t = ((x_here - x_index[:, None]) % n_x * n_core + (c_here + c_index[None, :]) % n_core).reshape(-1)
    mine_t = day[None].astype(jnp.int32)

    pieces = [mask_call(observed, direction, p, n_z) for p in range(probes)]

    space = entries_call(
        coords, tiles(mine_s, s_loc, tile_s), tiles(all_s, s_loc, tile_s), tile_s, space_range, STATIONS, "space_entries"
    )
    time = entries_call(
        day_features, tiles(all_t, t_loc, tile_t), tiles(mine_t, t_loc, tile_t), tile_t, time_range, DAYS, "time_entries"
    )

    def smooth_space(cells):
        return over_z(space_call(over_y(over_z(cells)), *space))

    def smooth_time(cells):
        return time_call(over_day(cells), *time)

    early = probes // 2
    outer = [smooth_time(smooth_space(pieces[p])) for p in range(early)]
    outer += [smooth_space(smooth_time(pieces[p])) for p in range(early, probes)]

    noise = noise[:, None]
    sums = [sums_call(observed, noise, residual, direction, outer[p], p) for p in range(probes)]
    first = over_all(jnp.concatenate(sums[:-1], axis=0))
    last = over_all(sums[-1])
    new = ()
    for p in range(probes):
        stats, row = (first, p) if p < probes - 1 else (last, 0)
        new = update_call(stats, row, observed, noise, solution, residual, direction, outer[p], p, new)
    return tuple(new)


def solution(mesh):
    in_specs = (
        P(None, "sta", "day"),
        P(None, "sta", "day"),
        P(None, "sta", "day"),
        P("sta", "day"),
        P(),
        P(),
        P("sta"),
    )
    out_specs = (P(None, "sta", "day"), P(None, "sta", "day"), P(None, "sta", "day"))
    return jax.shard_map(shards, mesh=mesh, in_specs=in_specs, out_specs=out_specs, check_vma=False)
```

```python
import functools
import math

import jax
import jax.numpy as jnp
from jax import lax
from jax.experimental import pallas as pl
from jax.experimental.pallas import tpu as pltpu
from jax.sharding import PartitionSpec as P

STATIONS = 4096
DAYS = 4096
FEAT = 4

space_range = 0.5
time_range = 0.5

HBM = pltpu.MemorySpace.HBM
F32 = jnp.float32
BF16 = jnp.bfloat16


class Chain:
    def __init__(self, place):
        self.place = place
        self.token = None

    def __call__(self, body, name, grid, operands, in_specs, outs, out_specs, scratch=(), aliases=()):
        operands, in_specs = list(operands), list(in_specs)
        n_in, n_tok = len(operands), 0 if self.token is None else 1
        if n_tok:
            operands.append(self.token)
            in_specs.append(pl.BlockSpec(memory_space=HBM))
        n_out = len(outs)

        def kernel(place, *refs):
            rest = refs[n_in + n_tok :]
            body(place, *refs[:n_in], *rest[:n_out], *rest[n_out + 1 :])

        found = pl.pallas_call(
            kernel,
            grid_spec=pltpu.PrefetchScalarGridSpec(
                num_scalar_prefetch=1,
                grid=grid,
                in_specs=in_specs,
                out_specs=list(out_specs) + [pl.BlockSpec(memory_space=HBM)],
                scratch_shapes=list(scratch),
            ),
            out_shape=[jax.ShapeDtypeStruct(*out) for out in outs] + [jax.ShapeDtypeStruct((8, 128), F32)],
            input_output_aliases={1 + k: v for k, v in aliases},
            compiler_params=pltpu.CompilerParams(vmem_limit_bytes=60 << 20),
            cost_estimate=pl.CostEstimate(flops=0, bytes_accessed=0, transcendentals=0),
            name=name,
        )(self.place, *operands)
        self.token = found[-1]
        return list(found[:-1])


def rows_spec(*shape):
    lead = len(shape) - 2
    return pl.BlockSpec(shape, lambda i, place: (0,) * lead + (i, 0))


def columns_of(place, k, sign, parts, width):
    block = lax.rem(place[0] + (k if sign > 0 else parts - k), parts)
    return pl.ds(pl.multiple_of(block * width, width), width)


CHUNKS = 4


def mask_call(chain, observed, direction, probe, parts, together):
    _, s_loc, t_loc = direction.shape
    width, rows = t_loc // parts, s_loc // CHUNKS

    def body(place, seen, way, *out):
        for k in range(parts):
            if together:
                at = pl.ds(k * width, width)
                out[0][k] = seen[:, at].astype(F32) * way[0, :, at]
            else:
                at = columns_of(place, k, 1, parts, width)
                out[k][...] = seen[:, at].astype(F32) * way[0, :, at]

    if together:
        outs, specs = [((parts, s_loc, width), F32)], [rows_spec(parts, rows, width)]
    else:
        outs, specs = [((s_loc, width), F32)] * parts, [rows_spec(rows, width)] * parts
    found = chain(
        body,
        "mask",
        (CHUNKS,),
        (observed, direction),
        [rows_spec(rows, t_loc), pl.BlockSpec((1, rows, t_loc), lambda i, place: (probe, i, 0))],
        outs,
        specs,
    )
    return found[0] if together else found


def stack_call(chain, pieces):
    s_loc, width = pieces[0].shape
    parts, rows = len(pieces), s_loc // CHUNKS

    def body(place, *refs):
        for k in range(parts):
            refs[parts][lax.rem(place[0] + parts - k, parts)] = refs[k][...]

    return chain(
        body,
        "stack",
        (CHUNKS,),
        pieces,
        [rows_spec(rows, width)] * parts,
        [((parts, s_loc, width), F32)],
        [rows_spec(parts, rows, width)],
    )[0]


def add_call(chain, terms):
    parts, s_loc, width = terms[0].shape
    rows = s_loc // CHUNKS

    def body(place, *refs):
        for k in range(parts):
            block = lax.rem(place[0] + k, parts)
            total = refs[0][block]
            for term in refs[1 : len(terms)]:
                total = total + term[block]
            refs[len(terms) + k][...] = total

    return chain(
        body,
        "add",
        (CHUNKS,),
        terms,
        [rows_spec(parts, rows, width)] * len(terms),
        [((s_loc, width), F32)] * parts,
        [rows_spec(rows, width)] * parts,
    )


def gate_call(chain, array):
    hbm = pl.BlockSpec(memory_space=HBM)
    return chain(lambda place, a, b: None, "gate", (), [array], [hbm], [(array.shape, array.dtype)], [hbm], aliases=[(0, 0)])[0]


def entries_call(chain, table, unit, n_rows, n_cols, row_block, col_block, reach, order, name, halves=(0, 1), earlier=()):
    features = table.shape[0]
    shape = (n_rows * unit, n_cols * unit)
    half, of = halves
    row_units = max(1, math.gcd(n_rows // of, 1024 // unit))
    col_units = max(1, math.gcd(n_cols, 1024 // unit))
    tile = (row_units * unit, col_units * unit)
    count = n_rows // of // row_units
    first = half * count
    shift = math.log(2.0 / order**0.5)
    step = 16

    def body(place, *refs):
        rows, cols = refs[:row_units], refs[row_units : row_units + col_units]
        high, low, across, down = refs[-4:]
        for u in range(col_units):
            for feature in range(features):
                line = cols[u][feature : feature + 1, :] * (1.0 / reach)
                across[feature, :, u * unit : (u + 1) * unit] = jnp.broadcast_to(line, (8, unit))
        for u in range(row_units):
            turned = jnp.concatenate([rows[u][...], jnp.zeros((8 - features, unit), F32)], axis=0).T * (1.0 / reach)
            for feature in range(features):
                down[feature, u * unit : (u + 1) * unit, :] = jnp.broadcast_to(turned[:, feature : feature + 1], (unit, 128))

        @pl.loop(0, tile[0] // step)
        def _(index):
            at = pl.ds(pl.multiple_of(index * step, step), step)
            total = None
            for feature in range(features):
                mine = jnp.concatenate([down[feature, at, :]] * (tile[1] // 128), axis=1)
                other = jnp.concatenate([across[feature]] * (step // 8), axis=0)
                diff = mine - other
                total = diff * diff if total is None else total + diff * diff
            dist = total * lax.rsqrt(jnp.maximum(total, 1e-37))
            high[at, :], low[at, :] = split(jnp.exp(shift - dist))

    def row_spec(u):
        return pl.BlockSpec((features, unit), lambda i, j, place: (0, row_block(place, (i + first) * row_units + u)))

    def col_spec(u):
        return pl.BlockSpec((features, unit), lambda i, j, place: (0, col_block(place, j * col_units + u)))

    out = pl.BlockSpec(tile, lambda i, j, place: (i + first, j))
    operands = [table] * (row_units + col_units)
    return chain(
        body,
        name,
        (count, n_cols // col_units),
        operands + list(earlier),
        [row_spec(u) for u in range(row_units)]
        + [col_spec(u) for u in range(col_units)]
        + [pl.BlockSpec(memory_space=HBM)] * len(earlier),
        [(shape, BF16)] * 2,
        [out, out],
        scratch=[pltpu.VMEM((features, 8, tile[1]), F32), pltpu.VMEM((features, tile[0], 128), F32)],
        aliases=[(len(operands) + k, k) for k in range(len(earlier))],
    )


def split(value):
    top = value.astype(BF16)
    return top, (value - top.astype(F32)).astype(BF16)


def dot(a, b):
    return jnp.dot(a, b, preferred_element_type=F32)


def space_call(chain, cells, matrices, together):
    parts, s_loc, width = cells[0].shape
    count = len(cells)
    span = parts * s_loc

    def body(place, *refs):
        mine, kern = refs[:count], refs[count : 3 * count]
        out, (cells_high, cells_low) = refs[3 * count : -2], refs[-2:]
        step = pl.program_id(0)

        @pl.when(step == 0)
        def _():
            for n in range(count):
                for b in range(parts):
                    at = pl.ds((n * parts + b) * s_loc, s_loc)
                    cells_high[at, :], cells_low[at, :] = split(mine[n][b])

        total = None
        for n in range(count):
            at = pl.ds(n * span, span)
            high, low = kern[2 * n], kern[2 * n + 1]
            term = dot(high[...], cells_high[at, :]) + dot(high[...], cells_low[at, :]) + dot(low[...], cells_high[at, :])
            total = term if total is None else total + term
        if together:
            out[0][0] = total
        else:
            for k in range(parts):

                @pl.when(step == k)
                def _():
                    out[k][...] = total

    whole = pl.BlockSpec((parts, s_loc, width), lambda i, place: (0, 0, 0))
    if together:
        matrix = pl.BlockSpec((s_loc, span), lambda i, place: (i, 0))
        outs, specs = [((parts, s_loc, width), F32)], [pl.BlockSpec((1, s_loc, width), lambda i, place: (i, 0, 0))]
    else:
        matrix = pl.BlockSpec((s_loc, span), lambda i, place: (lax.rem(place[0] + i, parts), 0))
        outs, specs = [((s_loc, width), F32)] * parts, [pl.BlockSpec((s_loc, width), lambda i, place: (0, 0))] * parts
    found = chain(
        body,
        "space",
        (parts,),
        list(cells) + [m for pair in matrices for m in pair],
        [whole] * count + [matrix] * (2 * count),
        outs,
        specs,
        scratch=[pltpu.VMEM((count * span, width), BF16)] * 2,
    )
    return found[0] if together else found


def time_call(chain, cells, matrix, cores):
    parts, s_loc, width = cells[0].shape
    count = len(cells)
    days = count * parts * width
    each = math.gcd(parts, 2)
    steps = parts // each

    def body(place, *refs):
        mine, (high, low) = refs[:count], refs[count : count + 2]
        out, (cells_high, cells_low) = refs[count + 2 : -2], refs[-2:]
        step = pl.program_id(0)

        @pl.when(step == 0)
        def _():
            for n in range(count):
                for b in range(parts):
                    at = pl.ds((n * parts + b) * width, width)
                    cells_high[:, at], cells_low[:, at] = split(mine[n][b])

        total = dot(cells_high[...], high[...]) + dot(cells_low[...], high[...]) + dot(cells_high[...], low[...])
        for c in range(cores):

            @pl.when(step // steps == c)
            def _():
                for e in range(each):
                    out[c][e] = total[:, e * width : (e + 1) * width]

    def out_spec(c):
        return pl.BlockSpec(
            (each, s_loc, width), lambda i, place: (jnp.clip(i - c * steps, 0, steps - 1), 0, 0)
        )

    whole = pl.BlockSpec((parts, s_loc, width), lambda i, place: (0, 0, 0))
    columns = pl.BlockSpec((days, each * width), lambda i, place: (0, i))
    return chain(
        body,
        "time",
        (steps * cores,),
        list(cells) + list(matrix),
        [whole] * count + [columns] * 2,
        [((parts, s_loc, width), F32)] * cores,
        [out_spec(c) for c in range(cores)],
        scratch=[pltpu.VMEM((s_loc, days), BF16)] * 2,
    )


class Outer:
    def __init__(self, refs):
        self.operands = list(refs)
        self.whole = refs[0].ndim == 3
        self.parts = refs[0].shape[0] if self.whole else len(refs)
        self.width = refs[0].shape[-1]

    def specs(self, rows):
        one = rows_spec(self.parts, rows, self.width) if self.whole else rows_spec(rows, self.width)
        return [one] * len(self.operands)

    def each(self, place, refs):
        for k in range(self.parts):
            if self.whole:
                value = refs[0][k]
                for other in refs[1:]:
                    value = value + other[k]
                yield pl.ds(k * self.width, self.width), value
            else:
                yield columns_of(place, k, -1, self.parts, self.width), refs[k][...]


def sums_call(chain, observed, noise, residual, direction, outer, probe):
    _, s_loc, t_loc = direction.shape
    rows = s_loc // CHUNKS
    n = len(outer.operands)

    def body(place, seen, var, res_ref, way_ref, *refs):
        out, total = refs[n:]
        step = pl.program_id(0)

        @pl.when(step == 0)
        def _():
            total[...] = jnp.zeros_like(total)

        for at, value in outer.each(place, refs[:n]):
            res, way = res_ref[0, :, at], way_ref[0, :, at]
            image = seen[:, at].astype(F32) * value + var[...] * way
            for row, product in enumerate((res * res, way * image, res * image, image * image)):
                total[row : row + 1, :] += jnp.sum(product, axis=0, keepdims=True)

        @pl.when(step == pl.num_programs(0) - 1)
        def _():
            out[...] = jnp.broadcast_to(jnp.sum(total[...], axis=1, keepdims=True), out.shape)

    probe_rows = pl.BlockSpec((1, rows, t_loc), lambda i, place: (probe, i, 0))
    return chain(
        body,
        "sums",
        (CHUNKS,),
        [observed, noise, residual, direction, *outer.operands],
        [rows_spec(rows, t_loc), rows_spec(rows, 1), probe_rows, probe_rows] + outer.specs(rows),
        [((8, 128), F32)],
        [pl.BlockSpec((8, 128), lambda i, place: (0, 0))],
        scratch=[pltpu.VMEM((8, outer.width), F32)],
    )[0]


def update_call(chain, stats, row, observed, noise, solution, residual, direction, outer, probe, earlier):
    _, s_loc, t_loc = direction.shape
    rows = s_loc // CHUNKS
    n = len(outer.operands)

    def body(place, given, seen, var, sol_ref, res_ref, way_ref, *refs):
        new_solution, new_residual, new_direction = refs[-3:]
        totals = jnp.sum(given[:, row * 8 : row * 8 + 8, :], axis=0)
        rr, pap, cross, square = (totals[k : k + 1, :1] for k in range(4))
        alpha = rr / pap
        rr_next = rr + alpha * (alpha * square - 2.0 * cross)
        beta = rr_next / rr
        for at, value in outer.each(place, refs[:n]):
            way = way_ref[0, :, at]
            image = seen[:, at].astype(F32) * value + var[...] * way
            fresh = res_ref[0, :, at] - alpha * image
            new_solution[0, :, at] = sol_ref[0, :, at] + alpha * way
            new_residual[0, :, at] = fresh
            new_direction[0, :, at] = fresh + beta * way

    probe_rows = pl.BlockSpec((1, rows, t_loc), lambda i, place: (probe, i, 0))
    operands = [stats, observed, noise, solution, residual, direction, *outer.operands]
    return chain(
        body,
        "update",
        (CHUNKS,),
        operands + list(earlier),
        [
            pl.BlockSpec(stats.shape, lambda i, place: (0, 0, 0)),
            rows_spec(rows, t_loc),
            rows_spec(rows, 1),
            probe_rows,
            probe_rows,
            probe_rows,
        ]
        + outer.specs(rows)
        + [pl.BlockSpec(memory_space=HBM)] * len(earlier),
        [(direction.shape, F32)] * 3,
        [probe_rows] * 3,
        aliases=[(len(operands) + k, k) for k in range(len(earlier))],
    )


def shards(solution, residual, direction, observed, coords, day_features, noise):
    n_sta = lax.axis_size("sta")
    n_day = lax.axis_size("day")
    _, s_loc, t_loc = direction.shape
    n_z = math.gcd(n_sta, 4)
    n_y = n_sta // n_z
    n_c = math.gcd(n_day, 2)
    n_x = n_day // n_c
    sta = lax.axis_index("sta")
    day = lax.axis_index("day")
    place = jnp.stack([sta // n_y, sta % n_y, day // n_c, day % n_c]).astype(jnp.int32)
    chain = Chain(place)

    def over_z(pieces):
        found = [pieces[0]]
        for k in range(1, n_z):
            pairs = [(z * n_y + y, (z + k) % n_z * n_y + y) for z in range(n_z) for y in range(n_y)]
            found.append(lax.ppermute(pieces[k], "sta", pairs))
        return found

    def over_z_at_once(pieces):
        groups = [[z * n_y + y for z in range(n_z)] for y in range(n_y)]
        return lax.all_to_all(pieces, "sta", 0, 0, axis_index_groups=groups, tiled=True)

    def over_y(cells):
        found = [cells]
        for k in range(1, n_y):
            pairs = [(z * n_y + y, z * n_y + (y + k) % n_y) for z in range(n_z) for y in range(n_y)]
            found.append(lax.ppermute(cells, "sta", pairs))
        return found

    def over_x(cells):
        found = [cells]
        for k in range(1, n_x):
            pairs = [(x * n_c + c, (x + k) % n_x * n_c + c) for x in range(n_x) for c in range(n_c)]
            found.append(lax.ppermute(cells, "day", pairs))
        return found

    def over_core(terms):
        pairs = [(j, j - j % n_c + (j + 1) % n_c) for j in range(n_day)]
        return terms[:1] + [lax.ppermute(term, "day", pairs) for term in terms[1:]]

    def over_all(*blocks):
        many = jnp.concatenate(blocks, axis=0) if len(blocks) > 1 else blocks[0]
        many = jnp.broadcast_to(many[None], (n_sta * n_day, *many.shape))
        return lax.all_to_all(many, ("sta", "day"), 0, 0, tiled=True)

    def back(value, k, size):
        return lax.rem(value + size - k, size)

    def space_row(place, i):
        return i * n_y + place[1]

    def space_col(shift):
        return lambda place, j: j * n_y + lax.rem(place[1] + n_y - shift, n_y)

    def time_row(place, i):
        return back(place[2], i, n_x) * n_c + place[3]

    def time_col(place, j):
        return place[2] * n_c + lax.rem(place[3] + j, n_c)

    def space_entries(shift, halves, earlier):
        col = space_col(shift)
        return entries_call(
            chain, coords, s_loc, n_z, n_z, space_row, col, space_range, STATIONS, "space_entries", halves, earlier
        )

    def space(cells, together):
        return space_call(chain, cells, matrices, together)

    def days(arrived):
        return over_core(time_call(chain, arrived, time, n_c))

    noise = noise[:, None]

    def sums(outer, p):
        return sums_call(chain, observed, noise, residual, direction, outer, p)

    def update(stats, row, outer, p, earlier):
        return update_call(chain, stats, row, observed, noise, solution, residual, direction, outer, p, earlier)

    def mask(p, together):
        return mask_call(chain, observed, direction, p, n_z, together)

    out0 = over_z(mask(0, False))
    x2 = over_x(mask(2, True))
    out1 = over_z_at_once(mask(1, True))
    time = entries_call(chain, day_features, t_loc, n_x, n_c, time_row, time_col, time_range, DAYS, "time_entries")
    x3 = over_x(mask(3, True))
    out2 = over_z(add_call(chain, days(x2)))
    cells0 = over_y(stack_call(chain, out0))
    matrices = [space_entries(0, (0, 2), ())]
    cells1 = over_y(gate_call(chain, out1))
    out3 = days(x3)
    matrices[0] = space_entries(0, (1, 2), matrices[0])
    out3 = over_z(add_call(chain, out3))
    for k in range(1, n_y):
        matrices.append(space_entries(k, (0, 1), ()))
    cells2 = over_y(stack_call(chain, out2))
    home0 = over_z_at_once(space(cells0, True))
    cells3 = over_y(stack_call(chain, out3))
    home1 = over_z(space(cells1, False))
    x0 = over_x(gate_call(chain, home0))
    home2 = over_z_at_once(space(cells2, True))
    home3 = over_z(space(cells3, False))
    outer0 = days(x0)
    x1 = over_x(stack_call(chain, home1))
    outer0 = Outer(outer0)
    sums0 = sums(outer0, 0)
    outer2 = Outer([home2])
    stats02 = over_all(sums0, sums(outer2, 2))
    outer1 = days(x1)
    new = update(stats02, 0, outer0, 0, ())
    outer1 = Outer(outer1)
    stats1 = over_all(sums(outer1, 1))
    new = update(stats02, 1, outer2, 2, new)
    outer3 = Outer(home3)
    stats3 = over_all(sums(outer3, 3))
    new = update(stats1, 0, outer1, 1, new)
    new = update(stats3, 0, outer3, 3, new)
    return tuple(new)


def solution(mesh):
    in_specs = (
        P(None, "sta", "day"),
        P(None, "sta", "day"),
        P(None, "sta", "day"),
        P("sta", "day"),
        P(),
        P(),
        P("sta"),
    )
    out_specs = (P(None, "sta", "day"), P(None, "sta", "day"), P(None, "sta", "day"))
    return jax.shard_map(shards, mesh=mesh, in_specs=in_specs, out_specs=out_specs, check_vma=False)
```

```python
import functools
import math

import jax
import jax.numpy as jnp
from jax import lax
from jax.experimental import pallas as pl
from jax.experimental.pallas import tpu as pltpu
from jax.sharding import PartitionSpec as P

STATIONS = 4096
DAYS = 4096
FEAT = 4

space_range = 0.5
time_range = 0.5

HBM = pltpu.MemorySpace.HBM
F32 = jnp.float32
BF16 = jnp.bfloat16


class Chain:
    def __init__(self, place):
        self.place = place
        self.token = None

    def __call__(self, body, name, grid, operands, in_specs, outs, out_specs, scratch=(), aliases=(), bytes_hint=0):
        operands, in_specs = list(operands), list(in_specs)
        n_in, n_tok = len(operands), 0 if self.token is None else 1
        if n_tok:
            operands.append(self.token)
            in_specs.append(pl.BlockSpec(memory_space=HBM))
        n_out = len(outs)

        def kernel(place, *refs):
            rest = refs[n_in + n_tok :]
            body(place, *refs[:n_in], *rest[:n_out], *rest[n_out + 1 :])

        found = pl.pallas_call(
            kernel,
            grid_spec=pltpu.PrefetchScalarGridSpec(
                num_scalar_prefetch=1,
                grid=grid,
                in_specs=in_specs,
                out_specs=list(out_specs) + [pl.BlockSpec(memory_space=HBM)],
                scratch_shapes=list(scratch),
            ),
            out_shape=[jax.ShapeDtypeStruct(*out) for out in outs] + [jax.ShapeDtypeStruct((8, 128), F32)],
            input_output_aliases={1 + k: v for k, v in aliases},
            compiler_params=pltpu.CompilerParams(vmem_limit_bytes=60 << 20),
            cost_estimate=pl.CostEstimate(flops=1150*bytes_hint, bytes_accessed=bytes_hint, transcendentals=0),
            name=name,
        )(self.place, *operands)
        self.token = found[-1]
        return list(found[:-1])


def rows_spec(*shape):
    lead = len(shape) - 2
    return pl.BlockSpec(shape, lambda i, place: (0,) * lead + (i, 0))


def columns_of(place, k, sign, parts, width):
    block = lax.rem(place[0] + (k if sign > 0 else parts - k), parts)
    return pl.ds(pl.multiple_of(block * width, width), width)


CHUNKS = 4


def mask_call(chain, observed, direction, probe, parts, together):
    _, s_loc, t_loc = direction.shape
    width, rows = t_loc // parts, s_loc // CHUNKS

    def body(place, seen, way, *out):
        for k in range(parts):
            if together:
                at = pl.ds(k * width, width)
                out[0][k] = seen[:, at].astype(F32) * way[0, :, at]
            else:
                at = columns_of(place, k, 1, parts, width)
                out[k][...] = seen[:, at].astype(F32) * way[0, :, at]

    if together:
        outs, specs = [((parts, s_loc, width), F32)], [rows_spec(parts, rows, width)]
    else:
        outs, specs = [((s_loc, width), F32)] * parts, [rows_spec(rows, width)] * parts
    found = chain(
        body,
        "mask",
        (CHUNKS,),
        (observed, direction),
        [rows_spec(rows, t_loc), pl.BlockSpec((1, rows, t_loc), lambda i, place: (probe, i, 0))],
        outs,
        specs,
    )
    return found[0] if together else found


def stack_call(chain, pieces):
    s_loc, width = pieces[0].shape
    parts, rows = len(pieces), s_loc // CHUNKS

    def body(place, *refs):
        for k in range(parts):
            refs[parts][lax.rem(place[0] + parts - k, parts)] = refs[k][...]

    return chain(
        body,
        "stack",
        (CHUNKS,),
        pieces,
        [rows_spec(rows, width)] * parts,
        [((parts, s_loc, width), F32)],
        [rows_spec(parts, rows, width)],
    )[0]


def add_call(chain, terms, together):
    parts, s_loc, width = terms[0].shape
    rows = s_loc // CHUNKS

    def body(place, *refs):
        for k in range(parts):
            block = k if together else lax.rem(place[0] + k, parts)
            total = refs[0][block]
            for term in refs[1 : len(terms)]:
                total = total + term[block]
            if together:
                refs[len(terms)][k] = total
            else:
                refs[len(terms) + k][...] = total

    if together:
        outs, specs = [((parts, s_loc, width), F32)], [rows_spec(parts, rows, width)]
    else:
        outs, specs = [((s_loc, width), F32)] * parts, [rows_spec(rows, width)] * parts
    found = chain(body, "add", (CHUNKS,), terms, [rows_spec(parts, rows, width)] * len(terms), outs, specs)
    return found[0] if together else found


def gate_call(chain, *arrays):
    anywhere = [pl.BlockSpec(memory_space=pl.ANY)] * len(arrays)
    outs = [(array.shape, array.dtype) for array in arrays]
    same = [(k, k) for k in range(len(arrays))]
    return chain(
        lambda place, *refs: None, "gate", (), arrays, anywhere, outs, anywhere, aliases=same, bytes_hint=20 << 20
    )


def entries_call(chain, table, unit, n_rows, n_cols, row_block, col_block, reach, order, name, halves=(0, 1), earlier=()):
    features = table.shape[0]
    shape = (n_rows * unit, n_cols * unit)
    half, of = halves
    row_units = max(1, math.gcd(n_rows // of, 1024 // unit))
    col_units = max(1, math.gcd(n_cols, 1024 // unit))
    tile = (row_units * unit, col_units * unit)
    count = n_rows // of // row_units
    first = half * count
    shift = math.log(2.0 / order**0.5)
    step = 16

    def body(place, *refs):
        rows, cols = refs[:row_units], refs[row_units : row_units + col_units]
        high, low, across, down = refs[-4:]
        for u in range(col_units):
            for feature in range(features):
                line = cols[u][feature : feature + 1, :] * (1.0 / reach)
                across[feature, :, u * unit : (u + 1) * unit] = jnp.broadcast_to(line, (8, unit))
        for u in range(row_units):
            turned = jnp.concatenate([rows[u][...], jnp.zeros((8 - features, unit), F32)], axis=0).T * (1.0 / reach)
            for feature in range(features):
                down[feature, u * unit : (u + 1) * unit, :] = jnp.broadcast_to(turned[:, feature : feature + 1], (unit, 128))

        @pl.loop(0, tile[0] // step)
        def _(index):
            at = pl.ds(pl.multiple_of(index * step, step), step)
            total = None
            for feature in range(features):
                mine = jnp.concatenate([down[feature, at, :]] * (tile[1] // 128), axis=1)
                other = jnp.concatenate([across[feature]] * (step // 8), axis=0)
                diff = mine - other
                total = diff * diff if total is None else total + diff * diff
            dist = total * lax.rsqrt(jnp.maximum(total, 1e-37))
            high[at, :], low[at, :] = split(jnp.exp(shift - dist))

    def row_spec(u):
        return pl.BlockSpec((features, unit), lambda i, j, place: (0, row_block(place, (i + first) * row_units + u)))

    def col_spec(u):
        return pl.BlockSpec((features, unit), lambda i, j, place: (0, col_block(place, j * col_units + u)))

    out = pl.BlockSpec(tile, lambda i, j, place: (i + first, j))
    operands = [table] * (row_units + col_units)
    return chain(
        body,
        name,
        (count, n_cols // col_units),
        operands + list(earlier),
        [row_spec(u) for u in range(row_units)]
        + [col_spec(u) for u in range(col_units)]
        + [pl.BlockSpec(memory_space=HBM)] * len(earlier),
        [(shape, BF16)] * 2,
        [out, out],
        scratch=[pltpu.VMEM((features, 8, tile[1]), F32), pltpu.VMEM((features, tile[0], 128), F32)],
        aliases=[(len(operands) + k, k) for k in range(len(earlier))],
    )


def split(value):
    top = value.astype(BF16)
    return top, (value - top.astype(F32)).astype(BF16)


def dot(a, b):
    return jnp.dot(a, b, preferred_element_type=F32)


def space_call(chain, cells, matrices, together):
    parts, s_loc, width = cells[0].shape
    count = len(cells)
    span = parts * s_loc

    def body(place, *refs):
        mine, kern = refs[:count], refs[count : 3 * count]
        out, (cells_high, cells_low) = refs[3 * count : -2], refs[-2:]
        step = pl.program_id(0)

        @pl.when(step == 0)
        def _():
            for n in range(count):
                for b in range(parts):
                    at = pl.ds((n * parts + b) * s_loc, s_loc)
                    cells_high[at, :], cells_low[at, :] = split(mine[n][b])

        total = None
        for n in range(count):
            at = pl.ds(n * span, span)
            high, low = kern[2 * n], kern[2 * n + 1]
            term = dot(high[...], cells_high[at, :]) + dot(high[...], cells_low[at, :]) + dot(low[...], cells_high[at, :])
            total = term if total is None else total + term
        if together:
            out[0][0] = total
        else:
            for k in range(parts):

                @pl.when(step == k)
                def _():
                    out[k][...] = total

    whole = pl.BlockSpec((parts, s_loc, width), lambda i, place: (0, 0, 0))
    if together:
        matrix = pl.BlockSpec((s_loc, span), lambda i, place: (i, 0))
        outs, specs = [((parts, s_loc, width), F32)], [pl.BlockSpec((1, s_loc, width), lambda i, place: (i, 0, 0))]
    else:
        matrix = pl.BlockSpec((s_loc, span), lambda i, place: (lax.rem(place[0] + i, parts), 0))
        outs, specs = [((s_loc, width), F32)] * parts, [pl.BlockSpec((s_loc, width), lambda i, place: (0, 0))] * parts
    found = chain(
        body,
        "space",
        (parts,),
        list(cells) + [m for pair in matrices for m in pair],
        [whole] * count + [matrix] * (2 * count),
        outs,
        specs,
        scratch=[pltpu.VMEM((count * span, width), BF16)] * 2,
    )
    return found[0] if together else found


def time_call(chain, cells, matrix, cores):
    parts, s_loc, width = cells[0].shape
    count = len(cells)
    days = count * parts * width
    each = math.gcd(parts, 2)
    steps = parts // each

    def body(place, *refs):
        mine, (high, low) = refs[:count], refs[count : count + 2]
        out, (cells_high, cells_low) = refs[count + 2 : -2], refs[-2:]
        step = pl.program_id(0)

        @pl.when(step == 0)
        def _():
            for n in range(count):
                for b in range(parts):
                    at = pl.ds((n * parts + b) * width, width)
                    cells_high[:, at], cells_low[:, at] = split(mine[n][b])

        total = dot(cells_high[...], high[...]) + dot(cells_low[...], high[...]) + dot(cells_high[...], low[...])
        for c in range(cores):

            @pl.when(step // steps == c)
            def _():
                for e in range(each):
                    out[c][e] = total[:, e * width : (e + 1) * width]

    def out_spec(c):
        return pl.BlockSpec(
            (each, s_loc, width), lambda i, place: (jnp.clip(i - c * steps, 0, steps - 1), 0, 0)
        )

    whole = pl.BlockSpec((parts, s_loc, width), lambda i, place: (0, 0, 0))
    columns = pl.BlockSpec((days, each * width), lambda i, place: (0, i))
    return chain(
        body,
        "time",
        (steps * cores,),
        list(cells) + list(matrix),
        [whole] * count + [columns] * 2,
        [((parts, s_loc, width), F32)] * cores,
        [out_spec(c) for c in range(cores)],
        scratch=[pltpu.VMEM((s_loc, days), BF16)] * 2,
    )


class Outer:
    def __init__(self, refs):
        self.operands = list(refs)
        self.whole = refs[0].ndim == 3
        self.parts = refs[0].shape[0] if self.whole else len(refs)
        self.width = refs[0].shape[-1]

    def specs(self, rows):
        one = rows_spec(self.parts, rows, self.width) if self.whole else rows_spec(rows, self.width)
        return [one] * len(self.operands)

    def each(self, place, refs):
        for k in range(self.parts):
            if self.whole:
                value = refs[0][k]
                for other in refs[1:]:
                    value = value + other[k]
                yield pl.ds(k * self.width, self.width), value
            else:
                yield columns_of(place, k, -1, self.parts, self.width), refs[k][...]


def sums_call(chain, observed, noise, residual, direction, outer, probe, bytes_hint=0):
    _, s_loc, t_loc = direction.shape
    rows = s_loc // CHUNKS
    n = len(outer.operands)

    def body(place, seen, var, res_ref, way_ref, *refs):
        out, total = refs[n:]
        step = pl.program_id(0)

        @pl.when(step == 0)
        def _():
            total[...] = jnp.zeros_like(total)

        for at, value in outer.each(place, refs[:n]):
            res, way = res_ref[0, :, at], way_ref[0, :, at]
            image = seen[:, at].astype(F32) * value + var[...] * way
            for row, product in enumerate((res * res, way * image, res * image, image * image)):
                total[row : row + 1, :] += jnp.sum(product, axis=0, keepdims=True)

        @pl.when(step == pl.num_programs(0) - 1)
        def _():
            out[...] = jnp.broadcast_to(jnp.sum(total[...], axis=1, keepdims=True), out.shape)

    probe_rows = pl.BlockSpec((1, rows, t_loc), lambda i, place: (probe, i, 0))
    return chain(
        body,
        "sums",
        (CHUNKS,),
        [observed, noise, residual, direction, *outer.operands],
        [rows_spec(rows, t_loc), rows_spec(rows, 1), probe_rows, probe_rows] + outer.specs(rows),
        [((8, 128), F32)],
        [pl.BlockSpec((8, 128), lambda i, place: (0, 0))],
        scratch=[pltpu.VMEM((8, outer.width), F32)],
        bytes_hint=bytes_hint,
    )[0]


def update_call(chain, stats, row, observed, noise, solution, residual, direction, outer, probe, earlier):
    _, s_loc, t_loc = direction.shape
    rows = s_loc // CHUNKS
    n = len(outer.operands)

    def body(place, given, seen, var, sol_ref, res_ref, way_ref, *refs):
        new_solution, new_residual, new_direction = refs[-3:]
        totals = jnp.sum(given[:, row * 8 : row * 8 + 8, :], axis=0)
        rr, pap, cross, square = (totals[k : k + 1, :1] for k in range(4))
        alpha = rr / pap
        rr_next = rr + alpha * (alpha * square - 2.0 * cross)
        beta = rr_next / rr
        for at, value in outer.each(place, refs[:n]):
            way = way_ref[0, :, at]
            image = seen[:, at].astype(F32) * value + var[...] * way
            fresh = res_ref[0, :, at] - alpha * image
            new_solution[0, :, at] = sol_ref[0, :, at] + alpha * way
            new_residual[0, :, at] = fresh
            new_direction[0, :, at] = fresh + beta * way

    probe_rows = pl.BlockSpec((1, rows, t_loc), lambda i, place: (probe, i, 0))
    operands = [stats, observed, noise, solution, residual, direction, *outer.operands]
    return chain(
        body,
        "update",
        (CHUNKS,),
        operands + list(earlier),
        [
            pl.BlockSpec(stats.shape, lambda i, place: (0, 0, 0)),
            rows_spec(rows, t_loc),
            rows_spec(rows, 1),
            probe_rows,
            probe_rows,
            probe_rows,
        ]
        + outer.specs(rows)
        + [pl.BlockSpec(memory_space=HBM)] * len(earlier),
        [(direction.shape, F32)] * 3,
        [probe_rows] * 3,
        aliases=[(len(operands) + k, k) for k in range(len(earlier))],
    )


def shards(solution, residual, direction, observed, coords, day_features, noise):
    n_sta = lax.axis_size("sta")
    n_day = lax.axis_size("day")
    _, s_loc, t_loc = direction.shape
    n_z = math.gcd(n_sta, 4)
    n_y = n_sta // n_z
    n_c = math.gcd(n_day, 2)
    n_x = n_day // n_c
    sta = lax.axis_index("sta")
    day = lax.axis_index("day")
    place = jnp.stack([sta // n_y, sta % n_y, day // n_c, day % n_c]).astype(jnp.int32)
    chain = Chain(place)

    def over_z(pieces):
        found = [pieces[0]]
        for k in range(1, n_z):
            pairs = [(z * n_y + y, (z + k) % n_z * n_y + y) for z in range(n_z) for y in range(n_y)]
            found.append(lax.ppermute(pieces[k], "sta", pairs))
        return found

    def over_z_at_once(pieces):
        groups = [[z * n_y + y for z in range(n_z)] for y in range(n_y)]
        return lax.all_to_all(pieces, "sta", 0, 0, axis_index_groups=groups, tiled=True)

    def over_y(cells):
        found = [cells]
        for k in range(1, n_y):
            pairs = [(z * n_y + y, z * n_y + (y + k) % n_y) for z in range(n_z) for y in range(n_y)]
            found.append(lax.ppermute(cells, "sta", pairs))
        return found

    def over_x(cells):
        found = [cells]
        for k in range(1, n_x):
            pairs = [(x * n_c + c, (x + k) % n_x * n_c + c) for x in range(n_x) for c in range(n_c)]
            found.append(lax.ppermute(cells, "day", pairs))
        return found

    def over_core(terms):
        pairs = [(j, j - j % n_c + (j + 1) % n_c) for j in range(n_day)]
        return terms[:1] + [lax.ppermute(term, "day", pairs) for term in terms[1:]]

    def over_all(*blocks):
        many = jnp.concatenate(blocks, axis=0) if len(blocks) > 1 else blocks[0]
        many = jnp.broadcast_to(many[None], (n_sta * n_day, *many.shape))
        return lax.all_to_all(many, ("sta", "day"), 0, 0, tiled=True)

    def back(value, k, size):
        return lax.rem(value + size - k, size)

    def space_row(place, i):
        return i * n_y + place[1]

    def space_col(shift):
        return lambda place, j: j * n_y + lax.rem(place[1] + n_y - shift, n_y)

    def time_row(place, i):
        return back(place[2], i, n_x) * n_c + place[3]

    def time_col(place, j):
        return place[2] * n_c + lax.rem(place[3] + j, n_c)

    def space_entries(shift, halves, earlier):
        col = space_col(shift)
        return entries_call(
            chain, coords, s_loc, n_z, n_z, space_row, col, space_range, STATIONS, "space_entries", halves, earlier
        )

    def space(cells, together):
        return space_call(chain, cells, matrices, together)

    def days(arrived):
        return over_core(time_call(chain, arrived, time, n_c))

    noise = noise[:, None]

    def sums(outer, p, hint=0):
        return sums_call(chain, observed, noise, residual, direction, outer, p, hint)

    def update(stats, row, outer, p, earlier):
        return update_call(chain, stats, row, observed, noise, solution, residual, direction, outer, p, earlier)

    def mask(p, together):
        return mask_call(chain, observed, direction, p, n_z, together)

    def pass_on(*groups):
        flat = iter(gate_call(chain, *[array for group in groups for array in group]))
        return [[next(flat) for _ in group] for group in groups]

    mask0 = mask(0, False)
    mask2 = mask(2, True)
    out0 = over_z(mask0)
    x2 = over_x(mask2)
    mask1 = mask(1, True)
    mask3 = mask(3, True)
    time = entries_call(chain, day_features, t_loc, n_x, n_c, time_row, time_col, time_range, DAYS, "time_entries")
    matrices = [space_entries(0, (0, 1), ())]
    cells0 = stack_call(chain, out0)
    (mask1,), (mask3,), x2 = pass_on([mask1], [mask3], x2[1:])

    out1 = over_z_at_once(mask1)
    x3 = over_x(mask3)
    y0 = over_y(cells0)
    terms2 = time_call(chain, [mask2] + x2, time, n_c)
    for k in range(1, n_y):
        matrices.append(space_entries(k, (0, 1), ()))
    x3, y0 = pass_on(x3[1:], y0[1:])
    inner2 = add_call(chain, over_core(terms2), True)
    (cells1,), (inner2,) = pass_on([out1], [inner2])

    out2 = over_z_at_once(inner2)
    y1 = over_y(cells1)
    terms3 = time_call(chain, [mask3] + x3, time, n_c)
    smooth0 = space([cells0] + y0, False)
    (y1,) = pass_on(y1[1:])
    inner3 = add_call(chain, over_core(terms3), False)
    (cells2,), inner3, smooth0 = pass_on([out2], inner3, smooth0)

    out3 = over_z(inner3)
    y2 = over_y(cells2)
    smooth1 = space([cells1] + y1, False)
    cells3 = stack_call(chain, out3)
    y2, smooth0, smooth1 = pass_on(y2[1:], smooth0, smooth1)

    home0 = over_z(smooth0)
    y3 = over_y(cells3)
    smooth2 = space([cells2] + y2, False)
    home0 = stack_call(chain, home0)
    y3, smooth1, smooth2 = pass_on(y3[1:], smooth1, smooth2)

    home1 = over_z(smooth1)
    x0 = over_x(home0)
    smooth3 = space([cells3] + y3, False)
    home1 = stack_call(chain, home1)
    x0, smooth2, smooth3 = pass_on(x0[1:], smooth2, smooth3)

    home2 = over_z(smooth2)
    x1 = over_x(home1)
    terms0 = time_call(chain, [home0] + x0, time, n_c)
    home2, x1, terms0, smooth3 = pass_on(home2, x1[1:], terms0, smooth3)

    home3 = over_z(smooth3)
    outer0 = Outer(over_core(terms0))
    outer2 = Outer(home2)
    sums2 = sums(outer2, 2)
    sums0 = sums(outer0, 0)
    terms1 = time_call(chain, [home1] + x1, time, n_c)
    outer1 = Outer(over_core(terms1))
    outer3 = Outer(home3)
    sums3 = sums(outer3, 3, 200 << 20)
    sums1 = sums(outer1, 1)
    stats = over_all(sums0, sums1, sums2, sums3)
    new = ()
    for p, outer in enumerate((outer0, outer1, outer2, outer3)):
        new = update(stats, p, outer, p, new)
    return tuple(new)


def solution(mesh):
    in_specs = (
        P(None, "sta", "day"),
        P(None, "sta", "day"),
        P(None, "sta", "day"),
        P("sta", "day"),
        P(),
        P(),
        P("sta"),
    )
    out_specs = (P(None, "sta", "day"), P(None, "sta", "day"), P(None, "sta", "day"))
    return jax.shard_map(shards, mesh=mesh, in_specs=in_specs, out_specs=out_specs, check_vma=False)
```

```python
import functools
import math

import jax
import jax.numpy as jnp
from jax import lax
from jax.experimental import pallas as pl
from jax.experimental.pallas import tpu as pltpu
from jax.sharding import PartitionSpec as P

STATIONS = 4096
DAYS = 4096
FEAT = 4

space_range = 0.5
time_range = 0.5

HBM = pltpu.MemorySpace.HBM
F32 = jnp.float32
BF16 = jnp.bfloat16


class Chain:
    def __init__(self, place):
        self.place = place
        self.token = None

    def __call__(self, body, name, grid, operands, in_specs, outs, out_specs, scratch=(), aliases=(), bytes_hint=0):
        operands, in_specs = list(operands), list(in_specs)
        n_in, n_tok = len(operands), 0 if self.token is None else 1
        if n_tok:
            operands.append(self.token)
            in_specs.append(pl.BlockSpec(memory_space=HBM))
        n_out = len(outs)

        def kernel(place, *refs):
            rest = refs[n_in + n_tok :]
            body(place, *refs[:n_in], *rest[:n_out], *rest[n_out + 1 :])

        found = pl.pallas_call(
            kernel,
            grid_spec=pltpu.PrefetchScalarGridSpec(
                num_scalar_prefetch=1,
                grid=grid,
                in_specs=in_specs,
                out_specs=list(out_specs) + [pl.BlockSpec(memory_space=HBM)],
                scratch_shapes=list(scratch),
            ),
            out_shape=[jax.ShapeDtypeStruct(*out) for out in outs] + [jax.ShapeDtypeStruct((8, 128), F32)],
            input_output_aliases={1 + k: v for k, v in aliases},
            compiler_params=pltpu.CompilerParams(vmem_limit_bytes=60 << 20),
            cost_estimate=pl.CostEstimate(flops=1150*bytes_hint, bytes_accessed=bytes_hint, transcendentals=0),
            name=name,
        )(self.place, *operands)
        self.token = found[-1]
        return list(found[:-1])


def rows_spec(*shape):
    lead = len(shape) - 2
    return pl.BlockSpec(shape, lambda i, place: (0,) * lead + (i, 0))


def columns_of(place, k, sign, parts, width):
    block = lax.rem(place[0] + (k if sign > 0 else parts - k), parts)
    return pl.ds(pl.multiple_of(block * width, width), width)


CHUNKS = 2


def mask_call(chain, observed, direction, probe, parts, together):
    _, s_loc, t_loc = direction.shape
    width, rows = t_loc // parts, s_loc // CHUNKS

    def body(place, seen, way, *out):
        for k in range(parts):
            if together:
                at = pl.ds(k * width, width)
                out[0][k] = seen[:, at].astype(F32) * way[0, :, at]
            else:
                at = columns_of(place, k, 1, parts, width)
                out[k][...] = seen[:, at].astype(F32) * way[0, :, at]

    if together:
        outs, specs = [((parts, s_loc, width), F32)], [rows_spec(parts, rows, width)]
    else:
        outs, specs = [((s_loc, width), F32)] * parts, [rows_spec(rows, width)] * parts
    found = chain(
        body,
        "mask",
        (CHUNKS,),
        (observed, direction),
        [
            rows_spec(rows, t_loc),
            pl.BlockSpec((1, rows, t_loc), lambda i, place: (probe, i, 0)),
        ],
        outs,
        specs,
    )
    return found[0] if together else found


def add_call(chain, terms, together):
    parts, s_loc, width = terms[0].shape
    rows = s_loc // CHUNKS

    def body(place, *refs):
        for k in range(parts):
            block = k if together else lax.rem(place[0] + k, parts)
            total = refs[0][block]
            for term in refs[1 : len(terms)]:
                total = total + term[block]
            if together:
                refs[len(terms)][k] = total
            else:
                refs[len(terms) + k][...] = total

    if together:
        outs, specs = [((parts, s_loc, width), F32)], [rows_spec(parts, rows, width)]
    else:
        outs, specs = [((s_loc, width), F32)] * parts, [rows_spec(rows, width)] * parts
    found = chain(body, "add", (CHUNKS,), terms, [rows_spec(parts, rows, width)] * len(terms), outs, specs)
    return found[0] if together else found


def gate_call(chain, arrays, pieces=()):
    n, parts = len(arrays), len(pieces)
    anywhere = pl.BlockSpec(memory_space=pl.ANY)
    outs = [(array.shape, array.dtype) for array in arrays]

    def body(place, *refs):
        if parts:
            given, whole, sems = refs[n : n + parts], refs[2 * n + parts], refs[-1]
            copies = []
            for k in range(parts):
                block = lax.rem(place[0] + parts - k, parts)
                copies.append(pltpu.make_async_copy(given[k], whole.at[block], sems.at[k]))
                copies[-1].start()
            for copy in copies:
                copy.wait()

    if parts:
        outs.append(((parts, *pieces[0].shape), F32))
    return chain(
        body,
        "gate",
        (),
        [*arrays, *pieces],
        [anywhere] * (n + parts),
        outs,
        [anywhere] * len(outs),
        scratch=[pltpu.SemaphoreType.DMA((parts,))] if parts else (),
        aliases=[(k, k) for k in range(n)],
        bytes_hint=20 << 20,
    )


def entries_call(chain, table, unit, n_rows, n_cols, row_block, col_block, reach, order, name, halves=(0, 1), earlier=()):
    features = table.shape[0]
    shape = (n_rows * unit, n_cols * unit)
    half, of = halves
    row_units = max(1, math.gcd(n_rows // of, 1024 // unit))
    col_units = max(1, math.gcd(n_cols, 1024 // unit))
    tile = (row_units * unit, col_units * unit)
    count = n_rows // of // row_units
    first = half * count
    shift = math.log(2.0 / order**0.5)
    step = 16

    def body(place, *refs):
        rows, cols = refs[:row_units], refs[row_units : row_units + col_units]
        high, low, across, down = refs[-4:]
        for u in range(col_units):
            for feature in range(features):
                line = cols[u][feature : feature + 1, :] * (1.0 / reach)
                across[feature, :, u * unit : (u + 1) * unit] = jnp.broadcast_to(line, (8, unit))
        for u in range(row_units):
            turned = jnp.concatenate([rows[u][...], jnp.zeros((8 - features, unit), F32)], axis=0).T * (1.0 / reach)
            for feature in range(features):
                down[feature, u * unit : (u + 1) * unit, :] = jnp.broadcast_to(turned[:, feature : feature + 1], (unit, 128))

        @pl.loop(0, tile[0] // step)
        def _(index):
            at = pl.ds(pl.multiple_of(index * step, step), step)
            total = None
            for feature in range(features):
                mine = jnp.concatenate([down[feature, at, :]] * (tile[1] // 128), axis=1)
                other = jnp.concatenate([across[feature]] * (step // 8), axis=0)
                diff = mine - other
                total = diff * diff if total is None else total + diff * diff
            dist = total * lax.rsqrt(jnp.maximum(total, 1e-37))
            high[at, :], low[at, :] = split(jnp.exp(shift - dist))

    def row_spec(u):
        return pl.BlockSpec((features, unit), lambda i, j, place: (0, row_block(place, (i + first) * row_units + u)))

    def col_spec(u):
        return pl.BlockSpec((features, unit), lambda i, j, place: (0, col_block(place, j * col_units + u)))

    out = pl.BlockSpec(tile, lambda i, j, place: (i + first, j))
    operands = [table] * (row_units + col_units)
    return chain(
        body,
        name,
        (count, n_cols // col_units),
        operands + list(earlier),
        [row_spec(u) for u in range(row_units)]
        + [col_spec(u) for u in range(col_units)]
        + [pl.BlockSpec(memory_space=HBM)] * len(earlier),
        [(shape, BF16)] * 2,
        [out, out],
        scratch=[pltpu.VMEM((features, 8, tile[1]), F32), pltpu.VMEM((features, tile[0], 128), F32)],
        aliases=[(len(operands) + k, k) for k in range(len(earlier))],
    )


def split(value):
    top = value.astype(BF16)
    return top, (value - top.astype(F32)).astype(BF16)


def dot(a, b):
    return jnp.dot(a, b, preferred_element_type=F32)


def space_call(chain, cells, matrices, together):
    parts, s_loc, width = cells[0].shape
    count = len(cells)
    span = parts * s_loc

    def body(place, *refs):
        mine, kern = refs[:count], refs[count : 3 * count]
        out, (cells_high, cells_low) = refs[3 * count : -2], refs[-2:]
        step = pl.program_id(0)

        @pl.when(step == 0)
        def _():
            for n in range(count):
                for b in range(parts):
                    at = pl.ds((n * parts + b) * s_loc, s_loc)
                    cells_high[at, :], cells_low[at, :] = split(mine[n][b])

        total = None
        for n in range(count):
            at = pl.ds(n * span, span)
            high, low = kern[2 * n], kern[2 * n + 1]
            term = dot(high[...], cells_high[at, :]) + dot(high[...], cells_low[at, :]) + dot(low[...], cells_high[at, :])
            total = term if total is None else total + term
        if together:
            out[0][0] = total
        else:
            for k in range(parts):

                @pl.when(step == k)
                def _():
                    out[k][...] = total

    whole = pl.BlockSpec((parts, s_loc, width), lambda i, place: (0, 0, 0))
    if together:
        matrix = pl.BlockSpec((s_loc, span), lambda i, place: (i, 0))
        outs, specs = [((parts, s_loc, width), F32)], [pl.BlockSpec((1, s_loc, width), lambda i, place: (i, 0, 0))]
    else:
        matrix = pl.BlockSpec((s_loc, span), lambda i, place: (lax.rem(place[0] + i, parts), 0))
        outs, specs = [((s_loc, width), F32)] * parts, [pl.BlockSpec((s_loc, width), lambda i, place: (0, 0))] * parts
    found = chain(
        body,
        "space",
        (parts,),
        list(cells) + [m for pair in matrices for m in pair],
        [whole] * count + [matrix] * (2 * count),
        outs,
        specs,
        scratch=[pltpu.VMEM((count * span, width), BF16)] * 2,
    )
    return found[0] if together else found


def time_call(chain, cells, matrix, cores):
    parts, s_loc, width = cells[0].shape
    count = len(cells)
    days = count * parts * width
    each = math.gcd(parts, 2)
    steps = parts // each

    def body(place, *refs):
        mine, (high, low) = refs[:count], refs[count : count + 2]
        out, (cells_high, cells_low) = refs[count + 2 : -2], refs[-2:]
        step = pl.program_id(0)

        @pl.when(step == 0)
        def _():
            for n in range(count):
                for b in range(parts):
                    at = pl.ds((n * parts + b) * width, width)
                    cells_high[:, at], cells_low[:, at] = split(mine[n][b])

        total = dot(cells_high[...], high[...]) + dot(cells_low[...], high[...]) + dot(cells_high[...], low[...])
        for c in range(cores):

            @pl.when(step // steps == c)
            def _():
                for e in range(each):
                    out[c][e] = total[:, e * width : (e + 1) * width]

    def out_spec(c):
        return pl.BlockSpec(
            (each, s_loc, width), lambda i, place: (jnp.clip(i - c * steps, 0, steps - 1), 0, 0)
        )

    whole = pl.BlockSpec((parts, s_loc, width), lambda i, place: (0, 0, 0))
    columns = pl.BlockSpec((days, each * width), lambda i, place: (0, i))
    return chain(
        body,
        "time",
        (steps * cores,),
        list(cells) + list(matrix),
        [whole] * count + [columns] * 2,
        [((parts, s_loc, width), F32)] * cores,
        [out_spec(c) for c in range(cores)],
        scratch=[pltpu.VMEM((s_loc, days), BF16)] * 2,
    )


class Outer:
    def __init__(self, refs):
        self.operands = list(refs)
        self.whole = refs[0].ndim == 3
        self.parts = refs[0].shape[0] if self.whole else len(refs)
        self.width = refs[0].shape[-1]

    def specs(self, rows):
        shape = (self.parts, rows, self.width) if self.whole else (rows, self.width)
        one = rows_spec(*shape)
        return [one] * len(self.operands)

    def each(self, place, refs):
        for k in range(self.parts):
            if self.whole:
                value = refs[0][k]
                for other in refs[1:]:
                    value = value + other[k]
                yield pl.ds(k * self.width, self.width), value
            else:
                yield columns_of(place, k, -1, self.parts, self.width), refs[k][...]


def sums_call(chain, observed, noise, residual, direction, outer, probe, bytes_hint=0):
    _, s_loc, t_loc = direction.shape
    rows = s_loc // CHUNKS
    n = len(outer.operands)

    def body(place, seen, var, res_ref, way_ref, *refs):
        out, total = refs[n:]
        step = pl.program_id(0)

        @pl.when(step == 0)
        def _():
            total[...] = jnp.zeros_like(total)

        for at, value in outer.each(place, refs[:n]):
            res, way = res_ref[0, :, at], way_ref[0, :, at]
            image = seen[:, at].astype(F32) * value + var[...] * way
            for row, product in enumerate((res * res, way * image, res * image, image * image)):
                total[row : row + 1, :] += jnp.sum(product, axis=0, keepdims=True)

        @pl.when(step == pl.num_programs(0) - 1)
        def _():
            out[...] = jnp.broadcast_to(jnp.sum(total[...], axis=1, keepdims=True), out.shape)

    probe_rows = pl.BlockSpec((1, rows, t_loc), lambda i, place: (probe, i, 0))
    return chain(
        body,
        "sums",
        (CHUNKS,),
        [observed, noise, residual, direction, *outer.operands],
        [rows_spec(rows, t_loc), rows_spec(rows, 1), probe_rows, probe_rows] + outer.specs(rows),
        [((8, 128), F32)],
        [pl.BlockSpec((8, 128), lambda i, place: (0, 0))],
        scratch=[pltpu.VMEM((8, outer.width), F32)],
        bytes_hint=bytes_hint,
    )[0]


def update_call(chain, stats, observed, noise, solution, residual, direction, outers):
    probes, s_loc, t_loc = direction.shape
    rows = s_loc // CHUNKS

    def body(place, given, seen, var, sol_ref, res_ref, way_ref, *refs):
        new_solution, new_residual, new_direction = refs[-3:]
        taken = 0
        for p, outer in enumerate(outers):
            mine = refs[taken : taken + len(outer.operands)]
            taken += len(outer.operands)

            @pl.when(pl.program_id(0) // CHUNKS == p)
            def _():
                totals = jnp.sum(given[:, p * 8 : p * 8 + 8, :], axis=0)
                rr, pap, cross, square = (totals[k : k + 1, :1] for k in range(4))
                alpha = rr / pap
                rr_next = rr + alpha * (alpha * square - 2.0 * cross)
                beta = rr_next / rr
                for at, value in outer.each(place, mine):
                    way = way_ref[0, :, at]
                    image = seen[:, at].astype(F32) * value + var[...] * way
                    fresh = res_ref[0, :, at] - alpha * image
                    new_solution[0, :, at] = sol_ref[0, :, at] + alpha * way
                    new_residual[0, :, at] = fresh
                    new_direction[0, :, at] = fresh + beta * way

    def outer_specs(p, outer):
        def row(i):
            return jnp.clip(i - p * CHUNKS, 0, CHUNKS - 1)

        if outer.whole:
            one = pl.BlockSpec((outer.parts, rows, outer.width), lambda i, place: (0, row(i), 0))
        else:
            one = pl.BlockSpec((rows, outer.width), lambda i, place: (row(i), 0))
        return [one] * len(outer.operands)

    probe_rows = pl.BlockSpec((1, rows, t_loc), lambda i, place: (i // CHUNKS, i % CHUNKS, 0))
    return chain(
        body,
        "update",
        (probes * CHUNKS,),
        [stats, observed, noise, solution, residual, direction] + [ref for outer in outers for ref in outer.operands],
        [
            pl.BlockSpec(stats.shape, lambda i, place: (0, 0, 0)),
            pl.BlockSpec((rows, t_loc), lambda i, place: (i % CHUNKS, 0)),
            pl.BlockSpec((rows, 1), lambda i, place: (i % CHUNKS, 0)),
            probe_rows,
            probe_rows,
            probe_rows,
        ]
        + [spec for p, outer in enumerate(outers) for spec in outer_specs(p, outer)],
        [(direction.shape, F32)] * 3,
        [probe_rows] * 3,
    )


def shards(solution, residual, direction, observed, coords, day_features, noise):
    n_sta = lax.axis_size("sta")
    n_day = lax.axis_size("day")
    _, s_loc, t_loc = direction.shape
    n_z = math.gcd(n_sta, 4)
    n_y = n_sta // n_z
    n_c = math.gcd(n_day, 2)
    n_x = n_day // n_c
    sta = lax.axis_index("sta")
    day = lax.axis_index("day")
    place = jnp.stack([sta // n_y, sta % n_y, day // n_c, day % n_c]).astype(jnp.int32)
    chain = Chain(place)

    def over_z(pieces):
        found = [pieces[0]]
        for k in range(1, n_z):
            pairs = [(z * n_y + y, (z + k) % n_z * n_y + y) for z in range(n_z) for y in range(n_y)]
            found.append(lax.ppermute(pieces[k], "sta", pairs))
        return found

    def over_z_at_once(pieces):
        groups = [[z * n_y + y for z in range(n_z)] for y in range(n_y)]
        return lax.all_to_all(pieces, "sta", 0, 0, axis_index_groups=groups, tiled=True)

    def over_y(cells):
        found = [cells]
        for k in range(1, n_y):
            pairs = [(z * n_y + y, z * n_y + (y + k) % n_y) for z in range(n_z) for y in range(n_y)]
            found.append(lax.ppermute(cells, "sta", pairs))
        return found

    def over_x(cells):
        found = [cells]
        for k in range(1, n_x):
            pairs = [(x * n_c + c, (x + k) % n_x * n_c + c) for x in range(n_x) for c in range(n_c)]
            found.append(lax.ppermute(cells, "day", pairs))
        return found

    def over_core(terms):
        pairs = [(j, j - j % n_c + (j + 1) % n_c) for j in range(n_day)]
        return terms[:1] + [lax.ppermute(term, "day", pairs) for term in terms[1:]]

    def over_all(*blocks):
        many = jnp.concatenate(blocks, axis=0) if len(blocks) > 1 else blocks[0]
        many = jnp.broadcast_to(many[None], (n_sta * n_day, *many.shape))
        return lax.all_to_all(many, ("sta", "day"), 0, 0, tiled=True)

    def back(value, k, size):
        return lax.rem(value + size - k, size)

    def space_row(place, i):
        return i * n_y + place[1]

    def space_col(shift):
        return lambda place, j: j * n_y + lax.rem(place[1] + n_y - shift, n_y)

    def time_row(place, i):
        return back(place[2], i, n_x) * n_c + place[3]

    def time_col(place, j):
        return place[2] * n_c + lax.rem(place[3] + j, n_c)

    def space_entries(shift, halves, earlier):
        col = space_col(shift)
        return entries_call(
            chain, coords, s_loc, n_z, n_z, space_row, col, space_range, STATIONS, "space_entries", halves, earlier
        )

    def space(cells, together):
        return space_call(chain, cells, matrices, together)

    def days(arrived):
        return over_core(time_call(chain, arrived, time, n_c))

    noise = noise[:, None]

    def sums(outer, p, hint=0):
        return sums_call(chain, observed, noise, residual, direction, outer, p, hint)

    def mask(p, together):
        return mask_call(chain, observed, direction, p, n_z, together)

    def pass_on(*groups, pieces=()):
        found = gate_call(chain, [array for group in groups for array in group], pieces)
        flat = iter(found)
        kept = [[next(flat) for _ in group] for group in groups]
        return kept + [found[-1]] if pieces else kept

    mask0 = mask(0, False)
    mask2 = mask(2, True)
    out0 = over_z(mask0)
    x2 = over_x(mask2)
    mask1 = mask(1, True)
    mask3 = mask(3, True)
    time = entries_call(chain, day_features, t_loc, n_x, n_c, time_row, time_col, time_range, DAYS, "time_entries")
    (mask1,), (mask3,), x2, cells0 = pass_on([mask1], [mask3], x2[1:], pieces=out0)

    out1 = over_z_at_once(mask1)
    x3 = over_x(mask3)
    y0 = over_y(cells0)
    terms2 = time_call(chain, [mask2] + x2, time, n_c)
    matrices = [space_entries(0, (0, 1), ())]
    x3, y0 = pass_on(x3[1:], y0[1:])
    inner2 = add_call(chain, over_core(terms2), True)
    (cells1,), (inner2,) = pass_on([out1], [inner2])

    out2 = over_z_at_once(inner2)
    y1 = over_y(cells1)
    terms3 = time_call(chain, [mask3] + x3, time, n_c)
    for k in range(1, n_y):
        matrices.append(space_entries(k, (0, 1), ()))
    (y1,) = pass_on(y1[1:])
    inner3 = add_call(chain, over_core(terms3), False)
    (cells2,), inner3 = pass_on([out2], inner3)

    out3 = over_z(inner3)
    y2 = over_y(cells2)
    smooth0 = space([cells0] + y0, False)
    y2, smooth0, cells3 = pass_on(y2[1:], smooth0, pieces=out3)

    home0 = over_z(smooth0)
    y3 = over_y(cells3)
    smooth1 = space([cells1] + y1, False)
    y3, smooth1, home0 = pass_on(y3[1:], smooth1, pieces=home0)

    home1 = over_z(smooth1)
    x0 = over_x(home0)
    smooth2 = space([cells2] + y2, False)
    x0, smooth2, home1 = pass_on(x0[1:], smooth2, pieces=home1)

    home2 = over_z(smooth2)
    x1 = over_x(home1)
    smooth3 = space([cells3] + y3, False)
    terms0 = time_call(chain, [home0] + x0, time, n_c)
    home2, x1, terms0, smooth3 = pass_on(home2, x1[1:], terms0, smooth3)

    home3 = over_z(smooth3)
    outer0 = Outer(over_core(terms0))
    outer2 = Outer(home2)
    sums2 = sums(outer2, 2)
    sums0 = sums(outer0, 0)
    terms1 = time_call(chain, [home1] + x1, time, n_c)
    outer1 = Outer(over_core(terms1))
    outer3 = Outer(home3)
    sums3 = sums(outer3, 3, 200 << 20)
    sums1 = sums(outer1, 1)
    stats = over_all(sums0, sums1, sums2, sums3)
    outers = (outer0, outer1, outer2, outer3)
    return tuple(update_call(chain, stats, observed, noise, solution, residual, direction, outers))


def solution(mesh):
    in_specs = (
        P(None, "sta", "day"),
        P(None, "sta", "day"),
        P(None, "sta", "day"),
        P("sta", "day"),
        P(),
        P(),
        P("sta"),
    )
    out_specs = (P(None, "sta", "day"), P(None, "sta", "day"), P(None, "sta", "day"))
    return jax.shard_map(shards, mesh=mesh, in_specs=in_specs, out_specs=out_specs, check_vma=False)
```

```python
import functools
import math

import jax
import jax.numpy as jnp
from jax import lax
from jax.experimental import pallas as pl
from jax.experimental.pallas import tpu as pltpu
from jax.sharding import PartitionSpec as P

STATIONS = 4096
DAYS = 4096
FEAT = 4

space_range = 0.5
time_range = 0.5

HBM = pltpu.MemorySpace.HBM
F32 = jnp.float32
BF16 = jnp.bfloat16


class Chain:
    def __init__(self, place):
        self.place = place
        self.token = None

    def __call__(self, body, name, grid, operands, in_specs, outs, out_specs, scratch=(), aliases=(), bytes_hint=0):
        operands, in_specs = list(operands), list(in_specs)
        n_in, n_tok = len(operands), 0 if self.token is None else 1
        if n_tok:
            operands.append(self.token)
            in_specs.append(pl.BlockSpec(memory_space=HBM))
        n_out = len(outs)

        def kernel(place, *refs):
            rest = refs[n_in + n_tok :]
            body(place, *refs[:n_in], *rest[:n_out], *rest[n_out + 1 :])

        found = pl.pallas_call(
            kernel,
            grid_spec=pltpu.PrefetchScalarGridSpec(
                num_scalar_prefetch=1,
                grid=grid,
                in_specs=in_specs,
                out_specs=list(out_specs) + [pl.BlockSpec(memory_space=HBM)],
                scratch_shapes=list(scratch),
            ),
            out_shape=[jax.ShapeDtypeStruct(*out) for out in outs] + [jax.ShapeDtypeStruct((8, 128), F32)],
            input_output_aliases={1 + k: v for k, v in aliases},
            compiler_params=pltpu.CompilerParams(vmem_limit_bytes=60 << 20),
            cost_estimate=pl.CostEstimate(flops=1150*bytes_hint, bytes_accessed=bytes_hint, transcendentals=0),
            name=name,
        )(self.place, *operands)
        self.token = found[-1]
        return list(found[:-1])


def rows_spec(*shape):
    lead = len(shape) - 2
    return pl.BlockSpec(shape, lambda i, place: (0,) * lead + (i, 0))


def columns_of(place, k, sign, parts, width):
    block = lax.rem(place[0] + (k if sign > 0 else parts - k), parts)
    return pl.ds(pl.multiple_of(block * width, width), width)


CHUNKS = 2


def mask_call(chain, observed, direction, probe, parts, together):
    _, s_loc, t_loc = direction.shape
    width, rows = t_loc // parts, s_loc // CHUNKS

    def body(place, seen, way, *out):
        for k in range(parts):
            if together:
                at = pl.ds(k * width, width)
                out[0][k] = seen[:, at].astype(F32) * way[0, :, at]
            else:
                at = columns_of(place, k, 1, parts, width)
                out[k][...] = seen[:, at].astype(F32) * way[0, :, at]

    if together:
        outs, specs = [((parts, s_loc, width), F32)], [rows_spec(parts, rows, width)]
    else:
        outs, specs = [((s_loc, width), F32)] * parts, [rows_spec(rows, width)] * parts
    found = chain(
        body,
        "mask",
        (CHUNKS,),
        (observed, direction),
        [
            rows_spec(rows, t_loc),
            pl.BlockSpec((1, rows, t_loc), lambda i, place: (probe, i, 0)),
        ],
        outs,
        specs,
    )
    return found[0] if together else found


def add_call(chain, terms, together):
    parts, s_loc, width = terms[0].shape
    rows = s_loc // CHUNKS

    def body(place, *refs):
        for k in range(parts):
            block = k if together else lax.rem(place[0] + k, parts)
            total = refs[0][block]
            for term in refs[1 : len(terms)]:
                total = total + term[block]
            if together:
                refs[len(terms)][k] = total
            else:
                refs[len(terms) + k][...] = total

    if together:
        outs, specs = [((parts, s_loc, width), F32)], [rows_spec(parts, rows, width)]
    else:
        outs, specs = [((s_loc, width), F32)] * parts, [rows_spec(rows, width)] * parts
    found = chain(body, "add", (CHUNKS,), terms, [rows_spec(parts, rows, width)] * len(terms), outs, specs)
    return found[0] if together else found


def gate_call(chain, arrays, pieces=(), hint=0):
    n, parts = len(arrays), len(pieces)
    anywhere = pl.BlockSpec(memory_space=pl.ANY)
    outs = [(array.shape, array.dtype) for array in arrays]

    def body(place, *refs):
        if parts:
            given, whole, (held, sems) = refs[n : n + parts], refs[2 * n + parts], refs[-2:]
            coming = [pltpu.make_async_copy(given[k], held.at[k], sems.at[k]) for k in range(parts)]
            for copy in coming:
                copy.start()
            going = []
            for k in range(parts):
                coming[k].wait()
                block = lax.rem(place[0] + parts - k, parts)
                going.append(pltpu.make_async_copy(held.at[k], whole.at[block], sems.at[parts + k]))
                going[k].start()
            for copy in going:
                copy.wait()

    if parts:
        outs.append(((parts, *pieces[0].shape), F32))
    return chain(
        body,
        "gate",
        (),
        [*arrays, *pieces],
        [anywhere] * (n + parts),
        outs,
        [anywhere] * len(outs),
        scratch=[pltpu.VMEM(outs[-1][0], F32), pltpu.SemaphoreType.DMA((2 * parts,))] if parts else (),
        aliases=[(k, k) for k in range(n)],
        bytes_hint=hint,
    )


def entries_call(chain, table, unit, n_rows, n_cols, row_block, col_block, reach, order, name, halves=(0, 1), earlier=()):
    features = table.shape[0]
    shape = (n_rows * unit, n_cols * unit)
    half, of = halves
    row_units = max(1, math.gcd(n_rows // of, 1024 // unit))
    col_units = max(1, math.gcd(n_cols, 1024 // unit))
    tile = (row_units * unit, col_units * unit)
    count = n_rows // of // row_units
    first = half * count
    shift = math.log(2.0 / order**0.5)
    step = 16

    def body(place, *refs):
        rows, cols = refs[:row_units], refs[row_units : row_units + col_units]
        high, low, across, down = refs[-4:]
        for u in range(col_units):
            for feature in range(features):
                line = cols[u][feature : feature + 1, :] * (1.0 / reach)
                across[feature, :, u * unit : (u + 1) * unit] = jnp.broadcast_to(line, (8, unit))
        for u in range(row_units):
            turned = jnp.concatenate([rows[u][...], jnp.zeros((8 - features, unit), F32)], axis=0).T * (1.0 / reach)
            for feature in range(features):
                down[feature, u * unit : (u + 1) * unit, :] = jnp.broadcast_to(turned[:, feature : feature + 1], (unit, 128))

        @pl.loop(0, tile[0] // step)
        def _(index):
            at = pl.ds(pl.multiple_of(index * step, step), step)
            total = None
            for feature in range(features):
                mine = jnp.concatenate([down[feature, at, :]] * (tile[1] // 128), axis=1)
                other = jnp.concatenate([across[feature]] * (step // 8), axis=0)
                diff = mine - other
                total = diff * diff if total is None else total + diff * diff
            dist = total * lax.rsqrt(jnp.maximum(total, 1e-37))
            high[at, :], low[at, :] = split(jnp.exp(shift - dist))

    def row_spec(u):
        return pl.BlockSpec((features, unit), lambda i, j, place: (0, row_block(place, (i + first) * row_units + u)))

    def col_spec(u):
        return pl.BlockSpec((features, unit), lambda i, j, place: (0, col_block(place, j * col_units + u)))

    out = pl.BlockSpec(tile, lambda i, j, place: (i + first, j))
    operands = [table] * (row_units + col_units)
    return chain(
        body,
        name,
        (count, n_cols // col_units),
        operands + list(earlier),
        [row_spec(u) for u in range(row_units)]
        + [col_spec(u) for u in range(col_units)]
        + [pl.BlockSpec(memory_space=HBM)] * len(earlier),
        [(shape, BF16)] * 2,
        [out, out],
        scratch=[pltpu.VMEM((features, 8, tile[1]), F32), pltpu.VMEM((features, tile[0], 128), F32)],
        aliases=[(len(operands) + k, k) for k in range(len(earlier))],
    )


def split(value):
    top = value.astype(BF16)
    return top, (value - top.astype(F32)).astype(BF16)


def dot(a, b):
    return jnp.dot(a, b, preferred_element_type=F32)


def space_call(chain, cells, matrices, together):
    parts, s_loc, width = cells[0].shape
    count = len(cells)
    span = parts * s_loc

    def body(place, *refs):
        mine, kern = refs[:count], refs[count : 3 * count]
        out, (cells_high, cells_low) = refs[3 * count : -2], refs[-2:]
        step = pl.program_id(0)

        @pl.when(step == 0)
        def _():
            for n in range(count):
                for b in range(parts):
                    at = pl.ds((n * parts + b) * s_loc, s_loc)
                    cells_high[at, :], cells_low[at, :] = split(mine[n][b])

        total = None
        for n in range(count):
            at = pl.ds(n * span, span)
            high, low = kern[2 * n], kern[2 * n + 1]
            term = dot(high[...], cells_high[at, :]) + dot(high[...], cells_low[at, :]) + dot(low[...], cells_high[at, :])
            total = term if total is None else total + term
        if together:
            out[0][0] = total
        else:
            for k in range(parts):

                @pl.when(step == k)
                def _():
                    out[k][...] = total

    whole = pl.BlockSpec((parts, s_loc, width), lambda i, place: (0, 0, 0))
    if together:
        matrix = pl.BlockSpec((s_loc, span), lambda i, place: (i, 0))
        outs, specs = [((parts, s_loc, width), F32)], [pl.BlockSpec((1, s_loc, width), lambda i, place: (i, 0, 0))]
    else:
        matrix = pl.BlockSpec((s_loc, span), lambda i, place: (lax.rem(place[0] + i, parts), 0))
        outs, specs = [((s_loc, width), F32)] * parts, [pl.BlockSpec((s_loc, width), lambda i, place: (0, 0))] * parts
    found = chain(
        body,
        "space",
        (parts,),
        list(cells) + [m for pair in matrices for m in pair],
        [whole] * count + [matrix] * (2 * count),
        outs,
        specs,
        scratch=[pltpu.VMEM((count * span, width), BF16)] * 2,
    )
    return found[0] if together else found


def time_call(chain, cells, matrix, cores):
    parts, s_loc, width = cells[0].shape
    count = len(cells)
    days = count * parts * width
    each = math.gcd(parts, 2)
    steps = parts // each

    def body(place, *refs):
        mine, (high, low) = refs[:count], refs[count : count + 2]
        out, (cells_high, cells_low) = refs[count + 2 : -2], refs[-2:]
        step = pl.program_id(0)

        @pl.when(step == 0)
        def _():
            for n in range(count):
                for b in range(parts):
                    at = pl.ds((n * parts + b) * width, width)
                    cells_high[:, at], cells_low[:, at] = split(mine[n][b])

        total = dot(cells_high[...], high[...]) + dot(cells_low[...], high[...]) + dot(cells_high[...], low[...])
        for c in range(cores):

            @pl.when(step // steps == c)
            def _():
                for e in range(each):
                    out[c][e] = total[:, e * width : (e + 1) * width]

    def out_spec(c):
        return pl.BlockSpec(
            (each, s_loc, width), lambda i, place: (jnp.clip(i - c * steps, 0, steps - 1), 0, 0)
        )

    whole = pl.BlockSpec((parts, s_loc, width), lambda i, place: (0, 0, 0))
    columns = pl.BlockSpec((days, each * width), lambda i, place: (0, i))
    return chain(
        body,
        "time",
        (steps * cores,),
        list(cells) + list(matrix),
        [whole] * count + [columns] * 2,
        [((parts, s_loc, width), F32)] * cores,
        [out_spec(c) for c in range(cores)],
        scratch=[pltpu.VMEM((s_loc, days), BF16)] * 2,
    )


class Outer:
    def __init__(self, refs):
        self.operands = list(refs)
        self.whole = refs[0].ndim == 3
        self.parts = refs[0].shape[0] if self.whole else len(refs)
        self.width = refs[0].shape[-1]

    def specs(self, rows):
        shape = (self.parts, rows, self.width) if self.whole else (rows, self.width)
        one = rows_spec(*shape)
        return [one] * len(self.operands)

    def each(self, place, refs):
        for k in range(self.parts):
            if self.whole:
                value = refs[0][k]
                for other in refs[1:]:
                    value = value + other[k]
                yield pl.ds(k * self.width, self.width), value
            else:
                yield columns_of(place, k, -1, self.parts, self.width), refs[k][...]


def sums_call(chain, observed, noise, residual, direction, outer, probe, bytes_hint=0):
    _, s_loc, t_loc = direction.shape
    rows = s_loc // CHUNKS
    n = len(outer.operands)

    def body(place, seen, var, res_ref, way_ref, *refs):
        out, total = refs[n:]
        step = pl.program_id(0)

        @pl.when(step == 0)
        def _():
            total[...] = jnp.zeros_like(total)

        for at, value in outer.each(place, refs[:n]):
            res, way = res_ref[0, :, at], way_ref[0, :, at]
            image = seen[:, at].astype(F32) * value + var[...] * way
            for row, product in enumerate((res * res, way * image, res * image, image * image)):
                total[row : row + 1, :] += jnp.sum(product, axis=0, keepdims=True)

        @pl.when(step == pl.num_programs(0) - 1)
        def _():
            out[...] = jnp.broadcast_to(jnp.sum(total[...], axis=1, keepdims=True), out.shape)

    probe_rows = pl.BlockSpec((1, rows, t_loc), lambda i, place: (probe, i, 0))
    return chain(
        body,
        "sums",
        (CHUNKS,),
        [observed, noise, residual, direction, *outer.operands],
        [rows_spec(rows, t_loc), rows_spec(rows, 1), probe_rows, probe_rows] + outer.specs(rows),
        [((8, 128), F32)],
        [pl.BlockSpec((8, 128), lambda i, place: (0, 0))],
        scratch=[pltpu.VMEM((8, outer.width), F32)],
        bytes_hint=bytes_hint,
    )[0]


def update_call(chain, stats, observed, noise, solution, residual, direction, outers):
    probes, s_loc, t_loc = direction.shape
    rows = s_loc // CHUNKS

    def body(place, given, seen, var, sol_ref, res_ref, way_ref, *refs):
        new_solution, new_residual, new_direction = refs[-3:]
        taken = 0
        for p, outer in enumerate(outers):
            mine = refs[taken : taken + len(outer.operands)]
            taken += len(outer.operands)

            @pl.when(pl.program_id(0) // CHUNKS == p)
            def _():
                totals = jnp.sum(given[:, p * 8 : p * 8 + 8, :], axis=0)
                rr, pap, cross, square = (totals[k : k + 1, :1] for k in range(4))
                alpha = rr / pap
                rr_next = rr + alpha * (alpha * square - 2.0 * cross)
                beta = rr_next / rr
                for at, value in outer.each(place, mine):
                    way = way_ref[0, :, at]
                    image = seen[:, at].astype(F32) * value + var[...] * way
                    fresh = res_ref[0, :, at] - alpha * image
                    new_solution[0, :, at] = sol_ref[0, :, at] + alpha * way
                    new_residual[0, :, at] = fresh
                    new_direction[0, :, at] = fresh + beta * way

    def outer_specs(p, outer):
        def row(i):
            return jnp.clip(i - p * CHUNKS, 0, CHUNKS - 1)

        if outer.whole:
            one = pl.BlockSpec((outer.parts, rows, outer.width), lambda i, place: (0, row(i), 0))
        else:
            one = pl.BlockSpec((rows, outer.width), lambda i, place: (row(i), 0))
        return [one] * len(outer.operands)

    probe_rows = pl.BlockSpec((1, rows, t_loc), lambda i, place: (i // CHUNKS, i % CHUNKS, 0))
    return chain(
        body,
        "update",
        (probes * CHUNKS,),
        [stats, observed, noise, solution, residual, direction] + [ref for outer in outers for ref in outer.operands],
        [
            pl.BlockSpec(stats.shape, lambda i, place: (0, 0, 0)),
            pl.BlockSpec((rows, t_loc), lambda i, place: (i % CHUNKS, 0)),
            pl.BlockSpec((rows, 1), lambda i, place: (i % CHUNKS, 0)),
            probe_rows,
            probe_rows,
            probe_rows,
        ]
        + [spec for p, outer in enumerate(outers) for spec in outer_specs(p, outer)],
        [(direction.shape, F32)] * 3,
        [probe_rows] * 3,
    )


def shards(solution, residual, direction, observed, coords, day_features, noise):
    n_sta = lax.axis_size("sta")
    n_day = lax.axis_size("day")
    _, s_loc, t_loc = direction.shape
    n_z = math.gcd(n_sta, 4)
    n_y = n_sta // n_z
    n_c = math.gcd(n_day, 2)
    n_x = n_day // n_c
    sta = lax.axis_index("sta")
    day = lax.axis_index("day")
    place = jnp.stack([sta // n_y, sta % n_y, day // n_c, day % n_c]).astype(jnp.int32)
    chain = Chain(place)

    def over_z(pieces):
        found = [pieces[0]]
        for k in range(1, n_z):
            pairs = [(z * n_y + y, (z + k) % n_z * n_y + y) for z in range(n_z) for y in range(n_y)]
            found.append(lax.ppermute(pieces[k], "sta", pairs))
        return found

    def over_z_at_once(pieces):
        groups = [[z * n_y + y for z in range(n_z)] for y in range(n_y)]
        return lax.all_to_all(pieces, "sta", 0, 0, axis_index_groups=groups, tiled=True)

    def over_y(cells):
        found = [cells]
        for k in range(1, n_y):
            pairs = [(z * n_y + y, z * n_y + (y + k) % n_y) for z in range(n_z) for y in range(n_y)]
            found.append(lax.ppermute(cells, "sta", pairs))
        return found

    def over_x(cells):
        found = [cells]
        for k in range(1, n_x):
            pairs = [(x * n_c + c, (x + k) % n_x * n_c + c) for x in range(n_x) for c in range(n_c)]
            found.append(lax.ppermute(cells, "day", pairs))
        return found

    def over_core(terms):
        pairs = [(j, j - j % n_c + (j + 1) % n_c) for j in range(n_day)]
        return terms[:1] + [lax.ppermute(term, "day", pairs) for term in terms[1:]]

    def over_all(*blocks):
        many = jnp.concatenate(blocks, axis=0) if len(blocks) > 1 else blocks[0]
        many = jnp.broadcast_to(many[None], (n_sta * n_day, *many.shape))
        return lax.all_to_all(many, ("sta", "day"), 0, 0, tiled=True)

    def back(value, k, size):
        return lax.rem(value + size - k, size)

    def space_row(place, i):
        return i * n_y + place[1]

    def space_col(shift):
        return lambda place, j: j * n_y + lax.rem(place[1] + n_y - shift, n_y)

    def time_row(place, i):
        return back(place[2], i, n_x) * n_c + place[3]

    def time_col(place, j):
        return place[2] * n_c + lax.rem(place[3] + j, n_c)

    def space_entries(shift, halves, earlier):
        col = space_col(shift)
        return entries_call(
            chain, coords, s_loc, n_z, n_z, space_row, col, space_range, STATIONS, "space_entries", halves, earlier
        )

    def space(cells, together):
        return space_call(chain, cells, matrices, together)

    def days(arrived):
        return over_core(time_call(chain, arrived, time, n_c))

    noise = noise[:, None]

    def sums(outer, p, hint=0):
        return sums_call(chain, observed, noise, residual, direction, outer, p, hint)

    def mask(p, together):
        return mask_call(chain, observed, direction, p, n_z, together)

    def pass_on(*groups, pieces=(), hint=0):
        found = gate_call(chain, [array for group in groups for array in group], pieces, hint)
        flat = iter(found)
        kept = [[next(flat) for _ in group] for group in groups]
        return kept + [found[-1]] if pieces else kept

    mask2 = mask(2, True)
    mask0 = mask(0, False)
    x2 = over_x(mask2)
    out0 = over_z(mask0)
    mask1 = mask(1, True)
    mask3 = mask(3, True)
    time = entries_call(chain, day_features, t_loc, n_x, n_c, time_row, time_col, time_range, DAYS, "time_entries")
    (mask1,), (mask3,), x2, cells0 = pass_on([mask1], [mask3], x2[1:], pieces=out0)

    out1 = over_z_at_once(mask1)
    x3 = over_x(mask3)
    y0 = over_y(cells0)
    terms2 = time_call(chain, [mask2] + x2, time, n_c)
    matrices = [space_entries(0, (0, 1), ())]
    x3, y0 = pass_on(x3[1:], y0[1:], hint=20 << 20)
    inner2 = add_call(chain, over_core(terms2), True)
    (cells1,), (inner2,) = pass_on([out1], [inner2])

    out2 = over_z_at_once(inner2)
    y1 = over_y(cells1)
    terms3 = time_call(chain, [mask3] + x3, time, n_c)
    for k in range(1, n_y):
        matrices.append(space_entries(k, (0, 1), ()))
    inner3 = add_call(chain, over_core(terms3), False)
    (cells2,), inner3 = pass_on([out2], inner3)

    out3 = over_z(inner3)
    y2 = over_y(cells2)
    smooth0 = space([cells0] + y0, False)
    smooth0, cells3 = pass_on(smooth0, pieces=out3)

    home0 = over_z(smooth0)
    y3 = over_y(cells3)
    smooth1 = space(y1, False)
    smooth1, home0 = pass_on(smooth1, pieces=home0)

    home1 = over_z(smooth1)
    x0 = over_x(home0)
    smooth2 = space(y2, False)
    smooth2, home1 = pass_on(smooth2, pieces=home1)

    home2 = over_z(smooth2)
    x1 = over_x(home1)
    smooth3 = space(y3, False)
    terms0 = time_call(chain, x0, time, n_c)
    home2, x1, terms0, smooth3 = pass_on(home2, x1[1:], terms0, smooth3)

    home3 = over_z(smooth3)
    outer0 = Outer(over_core(terms0))
    outer2 = Outer(home2)
    sums2 = sums(outer2, 2)
    sums0 = sums(outer0, 0)
    terms1 = time_call(chain, [home1] + x1, time, n_c)
    outer1 = Outer(over_core(terms1))
    outer3 = Outer(home3)
    sums3 = sums(outer3, 3, 200 << 20)
    sums1 = sums(outer1, 1)
    stats = over_all(sums0, sums1, sums2, sums3)
    outers = (outer0, outer1, outer2, outer3)
    return tuple(update_call(chain, stats, observed, noise, solution, residual, direction, outers))


def solution(mesh):
    in_specs = (
        P(None, "sta", "day"),
        P(None, "sta", "day"),
        P(None, "sta", "day"),
        P("sta", "day"),
        P(),
        P(),
        P("sta"),
    )
    out_specs = (P(None, "sta", "day"), P(None, "sta", "day"), P(None, "sta", "day"))
    return jax.shard_map(shards, mesh=mesh, in_specs=in_specs, out_specs=out_specs, check_vma=False)
```

```python
import functools
import math

import jax
import jax.numpy as jnp
from jax import lax
from jax.experimental import pallas as pl
from jax.experimental.pallas import tpu as pltpu
from jax.sharding import PartitionSpec as P

STATIONS = 4096
DAYS = 4096
FEAT = 4

space_range = 0.5
time_range = 0.5

HBM = pltpu.MemorySpace.HBM
F32 = jnp.float32
BF16 = jnp.bfloat16


class Chain:
    def __init__(self, place):
        self.place = place
        self.token = None

    def __call__(self, body, name, grid, operands, in_specs, outs, out_specs, scratch=(), aliases=(), bytes_hint=0):
        operands, in_specs = list(operands), list(in_specs)
        n_in, n_tok = len(operands), 0 if self.token is None else 1
        if n_tok:
            operands.append(self.token)
            in_specs.append(pl.BlockSpec(memory_space=HBM))
        n_out = len(outs)

        def kernel(place, *refs):
            rest = refs[n_in + n_tok :]
            body(place, *refs[:n_in], *rest[:n_out], *rest[n_out + 1 :])

        found = pl.pallas_call(
            kernel,
            grid_spec=pltpu.PrefetchScalarGridSpec(
                num_scalar_prefetch=1,
                grid=grid,
                in_specs=in_specs,
                out_specs=list(out_specs) + [pl.BlockSpec(memory_space=HBM)],
                scratch_shapes=list(scratch),
            ),
            out_shape=[jax.ShapeDtypeStruct(*out) for out in outs] + [jax.ShapeDtypeStruct((8, 128), F32)],
            input_output_aliases={1 + k: v for k, v in aliases},
            compiler_params=pltpu.CompilerParams(vmem_limit_bytes=60 << 20),
            cost_estimate=pl.CostEstimate(flops=1150*bytes_hint, bytes_accessed=bytes_hint, transcendentals=0),
            name=name,
        )(self.place, *operands)
        self.token = found[-1]
        return list(found[:-1])


def rows_spec(*shape):
    lead = len(shape) - 2
    return pl.BlockSpec(shape, lambda i, place: (0,) * lead + (i, 0))


def columns_of(place, k, sign, parts, width):
    block = lax.rem(place[0] + (k if sign > 0 else parts - k), parts)
    return pl.ds(pl.multiple_of(block * width, width), width)


CHUNKS = 2


def mask_call(chain, observed, direction, probe, parts, together):
    _, s_loc, t_loc = direction.shape
    width, rows = t_loc // parts, s_loc // CHUNKS

    def body(place, seen, way, *out):
        for k in range(parts):
            if together:
                at = pl.ds(k * width, width)
                out[0][k] = seen[:, at].astype(F32) * way[0, :, at]
            else:
                at = columns_of(place, k, 1, parts, width)
                out[k][...] = seen[:, at].astype(F32) * way[0, :, at]

    if together:
        outs, specs = [((parts, s_loc, width), F32)], [rows_spec(parts, rows, width)]
    else:
        outs, specs = [((s_loc, width), F32)] * parts, [rows_spec(rows, width)] * parts
    found = chain(
        body,
        "mask",
        (CHUNKS,),
        (observed, direction),
        [
            rows_spec(rows, t_loc),
            pl.BlockSpec((1, rows, t_loc), lambda i, place: (probe, i, 0)),
        ],
        outs,
        specs,
    )
    return found[0] if together else found


def add_call(chain, terms, together):
    parts, s_loc, width = terms[0].shape
    rows = s_loc // CHUNKS

    def body(place, *refs):
        for k in range(parts):
            block = k if together else lax.rem(place[0] + k, parts)
            total = refs[0][block]
            for term in refs[1 : len(terms)]:
                total = total + term[block]
            if together:
                refs[len(terms)][k] = total
            else:
                refs[len(terms) + k][...] = total

    if together:
        outs, specs = [((parts, s_loc, width), F32)], [rows_spec(parts, rows, width)]
    else:
        outs, specs = [((s_loc, width), F32)] * parts, [rows_spec(rows, width)] * parts
    found = chain(body, "add", (CHUNKS,), terms, [rows_spec(parts, rows, width)] * len(terms), outs, specs)
    return found[0] if together else found


def gate_call(chain, arrays, pieces=(), hint=0):
    n, parts = len(arrays), len(pieces)
    anywhere = pl.BlockSpec(memory_space=pl.ANY)
    outs = [(array.shape, array.dtype) for array in arrays]

    def body(place, *refs):
        if parts:
            given, whole, (held, sems) = refs[n : n + parts], refs[2 * n + parts], refs[-2:]
            coming = [pltpu.make_async_copy(given[k], held.at[k], sems.at[k]) for k in range(parts)]
            for copy in coming:
                copy.start()
            going = []
            for k in range(parts):
                coming[k].wait()
                block = lax.rem(place[0] + parts - k, parts)
                going.append(pltpu.make_async_copy(held.at[k], whole.at[block], sems.at[parts + k]))
                going[k].start()
            for copy in going:
                copy.wait()

    if parts:
        outs.append(((parts, *pieces[0].shape), F32))
    return chain(
        body,
        "gate",
        (),
        [*arrays, *pieces],
        [anywhere] * (n + parts),
        outs,
        [anywhere] * len(outs),
        scratch=[pltpu.VMEM(outs[-1][0], F32), pltpu.SemaphoreType.DMA((2 * parts,))] if parts else (),
        aliases=[(k, k) for k in range(n)],
        bytes_hint=hint,
    )


def entries_call(chain, table, unit, n_rows, n_cols, row_block, col_block, reach, order, name, halves=(0, 1), earlier=()):
    features = table.shape[0]
    shape = (n_rows * unit, n_cols * unit)
    half, of = halves
    row_units = max(1, math.gcd(n_rows // of, 1024 // unit))
    col_units = max(1, math.gcd(n_cols, 1024 // unit))
    tile = (row_units * unit, col_units * unit)
    count = n_rows // of // row_units
    first = half * count
    shift = math.log(2.0 / order**0.5)
    step = 16

    def body(place, *refs):
        rows, cols = refs[:row_units], refs[row_units : row_units + col_units]
        high, low, across, down = refs[-4:]
        for u in range(col_units):
            for feature in range(features):
                line = cols[u][feature : feature + 1, :] * (1.0 / reach)
                across[feature, :, u * unit : (u + 1) * unit] = jnp.broadcast_to(line, (8, unit))
        for u in range(row_units):
            turned = jnp.concatenate([rows[u][...], jnp.zeros((8 - features, unit), F32)], axis=0).T * (1.0 / reach)
            for feature in range(features):
                down[feature, u * unit : (u + 1) * unit, :] = jnp.broadcast_to(turned[:, feature : feature + 1], (unit, 128))

        @pl.loop(0, tile[0] // step)
        def _(index):
            at = pl.ds(pl.multiple_of(index * step, step), step)
            total = None
            for feature in range(features):
                mine = jnp.concatenate([down[feature, at, :]] * (tile[1] // 128), axis=1)
                other = jnp.concatenate([across[feature]] * (step // 8), axis=0)
                diff = mine - other
                total = diff * diff if total is None else total + diff * diff
            dist = total * lax.rsqrt(jnp.maximum(total, 1e-37))
            high[at, :], low[at, :] = split(jnp.exp(shift - dist))

    def row_spec(u):
        return pl.BlockSpec((features, unit), lambda i, j, place: (0, row_block(place, (i + first) * row_units + u)))

    def col_spec(u):
        return pl.BlockSpec((features, unit), lambda i, j, place: (0, col_block(place, j * col_units + u)))

    out = pl.BlockSpec(tile, lambda i, j, place: (i + first, j))
    operands = [table] * (row_units + col_units)
    return chain(
        body,
        name,
        (count, n_cols // col_units),
        operands + list(earlier),
        [row_spec(u) for u in range(row_units)]
        + [col_spec(u) for u in range(col_units)]
        + [pl.BlockSpec(memory_space=HBM)] * len(earlier),
        [(shape, BF16)] * 2,
        [out, out],
        scratch=[pltpu.VMEM((features, 8, tile[1]), F32), pltpu.VMEM((features, tile[0], 128), F32)],
        aliases=[(len(operands) + k, k) for k in range(len(earlier))],
    )


def split(value):
    top = value.astype(BF16)
    return top, (value - top.astype(F32)).astype(BF16)


def dot(a, b):
    return jnp.dot(a, b, preferred_element_type=F32)


def space_call(chain, cells, matrices, together):
    parts, s_loc, width = cells[0].shape
    count = len(cells)
    span = parts * s_loc

    def body(place, *refs):
        mine, kern = refs[:count], refs[count : 3 * count]
        out, (cells_high, cells_low) = refs[3 * count : -2], refs[-2:]
        step = pl.program_id(0)

        @pl.when(step == 0)
        def _():
            for n in range(count):
                for b in range(parts):
                    at = pl.ds((n * parts + b) * s_loc, s_loc)
                    cells_high[at, :], cells_low[at, :] = split(mine[n][b])

        total = None
        for n in range(count):
            at = pl.ds(n * span, span)
            high, low = kern[2 * n], kern[2 * n + 1]
            term = dot(high[...], cells_high[at, :]) + dot(high[...], cells_low[at, :]) + dot(low[...], cells_high[at, :])
            total = term if total is None else total + term
        if together:
            out[0][0] = total
        else:
            for k in range(parts):

                @pl.when(step == k)
                def _():
                    out[k][...] = total

    whole = pl.BlockSpec((parts, s_loc, width), lambda i, place: (0, 0, 0))
    if together:
        matrix = pl.BlockSpec((s_loc, span), lambda i, place: (i, 0))
        outs, specs = [((parts, s_loc, width), F32)], [pl.BlockSpec((1, s_loc, width), lambda i, place: (i, 0, 0))]
    else:
        matrix = pl.BlockSpec((s_loc, span), lambda i, place: (lax.rem(place[0] + i, parts), 0))
        outs, specs = [((s_loc, width), F32)] * parts, [pl.BlockSpec((s_loc, width), lambda i, place: (0, 0))] * parts
    found = chain(
        body,
        "space",
        (parts,),
        list(cells) + [m for pair in matrices for m in pair],
        [whole] * count + [matrix] * (2 * count),
        outs,
        specs,
        scratch=[pltpu.VMEM((count * span, width), BF16)] * 2,
    )
    return found[0] if together else found


def time_call(chain, cells, matrix, cores):
    parts, s_loc, width = cells[0].shape
    count = len(cells)
    days = count * parts * width
    each = math.gcd(parts, 2)
    steps = parts // each

    def body(place, *refs):
        mine, (high, low) = refs[:count], refs[count : count + 2]
        out, (cells_high, cells_low) = refs[count + 2 : -2], refs[-2:]
        step = pl.program_id(0)

        @pl.when(step == 0)
        def _():
            for n in range(count):
                for b in range(parts):
                    at = pl.ds((n * parts + b) * width, width)
                    cells_high[:, at], cells_low[:, at] = split(mine[n][b])

        total = dot(cells_high[...], high[...]) + dot(cells_low[...], high[...]) + dot(cells_high[...], low[...])
        for c in range(cores):

            @pl.when(step // steps == c)
            def _():
                for e in range(each):
                    out[c][e] = total[:, e * width : (e + 1) * width]

    def out_spec(c):
        return pl.BlockSpec(
            (each, s_loc, width), lambda i, place: (jnp.clip(i - c * steps, 0, steps - 1), 0, 0)
        )

    whole = pl.BlockSpec((parts, s_loc, width), lambda i, place: (0, 0, 0))
    columns = pl.BlockSpec((days, each * width), lambda i, place: (0, i))
    return chain(
        body,
        "time",
        (steps * cores,),
        list(cells) + list(matrix),
        [whole] * count + [columns] * 2,
        [((parts, s_loc, width), F32)] * cores,
        [out_spec(c) for c in range(cores)],
        scratch=[pltpu.VMEM((s_loc, days), BF16)] * 2,
    )


class Outer:
    def __init__(self, refs):
        self.operands = list(refs)
        self.whole = refs[0].ndim == 3
        self.parts = refs[0].shape[0] if self.whole else len(refs)
        self.width = refs[0].shape[-1]

    def specs(self, rows):
        shape = (self.parts, rows, self.width) if self.whole else (rows, self.width)
        one = rows_spec(*shape)
        return [one] * len(self.operands)

    def each(self, place, refs):
        for k in range(self.parts):
            if self.whole:
                value = refs[0][k]
                for other in refs[1:]:
                    value = value + other[k]
                yield pl.ds(k * self.width, self.width), value
            else:
                yield columns_of(place, k, -1, self.parts, self.width), refs[k][...]


def sums_call(chain, observed, noise, residual, direction, outer, probe, bytes_hint=0):
    _, s_loc, t_loc = direction.shape
    rows = s_loc // CHUNKS
    n = len(outer.operands)

    def body(place, seen, var, res_ref, way_ref, *refs):
        out, total = refs[n:]
        step = pl.program_id(0)

        @pl.when(step == 0)
        def _():
            total[...] = jnp.zeros_like(total)

        for at, value in outer.each(place, refs[:n]):
            res, way = res_ref[0, :, at], way_ref[0, :, at]
            image = seen[:, at].astype(F32) * value + var[...] * way
            for row, product in enumerate((res * res, way * image, res * image, image * image)):
                total[row : row + 1, :] += jnp.sum(product, axis=0, keepdims=True)

        @pl.when(step == pl.num_programs(0) - 1)
        def _():
            out[...] = jnp.broadcast_to(jnp.sum(total[...], axis=1, keepdims=True), out.shape)

    probe_rows = pl.BlockSpec((1, rows, t_loc), lambda i, place: (probe, i, 0))
    return chain(
        body,
        "sums",
        (CHUNKS,),
        [observed, noise, residual, direction, *outer.operands],
        [rows_spec(rows, t_loc), rows_spec(rows, 1), probe_rows, probe_rows] + outer.specs(rows),
        [((8, 128), F32)],
        [pl.BlockSpec((8, 128), lambda i, place: (0, 0))],
        scratch=[pltpu.VMEM((8, outer.width), F32)],
        bytes_hint=bytes_hint,
    )[0]


def update_call(chain, stats, observed, noise, solution, residual, direction, outers, first, earlier):
    _, s_loc, t_loc = direction.shape
    rows = s_loc // CHUNKS

    def body(place, given, seen, var, sol_ref, res_ref, way_ref, *refs):
        new_solution, new_residual, new_direction = refs[-3:]
        taken = 0
        for p, outer in enumerate(outers):
            mine = refs[taken : taken + len(outer.operands)]
            taken += len(outer.operands)

            @pl.when(pl.program_id(0) // CHUNKS == p)
            def _():
                totals = jnp.sum(given[:, p * 8 : p * 8 + 8, :], axis=0)
                rr, pap, cross, square = (totals[k : k + 1, :1] for k in range(4))
                alpha = rr / pap
                rr_next = rr + alpha * (alpha * square - 2.0 * cross)
                beta = rr_next / rr
                for at, value in outer.each(place, mine):
                    way = way_ref[0, :, at]
                    image = seen[:, at].astype(F32) * value + var[...] * way
                    fresh = res_ref[0, :, at] - alpha * image
                    new_solution[0, :, at] = sol_ref[0, :, at] + alpha * way
                    new_residual[0, :, at] = fresh
                    new_direction[0, :, at] = fresh + beta * way

    def outer_specs(p, outer):
        def row(i):
            return jnp.clip(i - p * CHUNKS, 0, CHUNKS - 1)

        if outer.whole:
            one = pl.BlockSpec((outer.parts, rows, outer.width), lambda i, place: (0, row(i), 0))
        else:
            one = pl.BlockSpec((rows, outer.width), lambda i, place: (row(i), 0))
        return [one] * len(outer.operands)

    probe_rows = pl.BlockSpec((1, rows, t_loc), lambda i, place: (i // CHUNKS * 2 + first, i % CHUNKS, 0))
    operands = [stats, observed, noise, solution, residual, direction]
    operands += [ref for outer in outers for ref in outer.operands]
    return chain(
        body,
        "update",
        (len(outers) * CHUNKS,),
        operands + list(earlier),
        [
            pl.BlockSpec(stats.shape, lambda i, place: (0, 0, 0)),
            pl.BlockSpec((rows, t_loc), lambda i, place: (i % CHUNKS, 0)),
            pl.BlockSpec((rows, 1), lambda i, place: (i % CHUNKS, 0)),
            probe_rows,
            probe_rows,
            probe_rows,
        ]
        + [spec for p, outer in enumerate(outers) for spec in outer_specs(p, outer)]
        + [pl.BlockSpec(memory_space=HBM)] * len(earlier),
        [(direction.shape, F32)] * 3,
        [probe_rows] * 3,
        aliases=[(len(operands) + k, k) for k in range(len(earlier))],
    )


def shards(solution, residual, direction, observed, coords, day_features, noise):
    n_sta = lax.axis_size("sta")
    n_day = lax.axis_size("day")
    _, s_loc, t_loc = direction.shape
    n_z = math.gcd(n_sta, 4)
    n_y = n_sta // n_z
    n_c = math.gcd(n_day, 2)
    n_x = n_day // n_c
    sta = lax.axis_index("sta")
    day = lax.axis_index("day")
    place = jnp.stack([sta // n_y, sta % n_y, day // n_c, day % n_c]).astype(jnp.int32)
    chain = Chain(place)

    def over_z(pieces):
        found = [pieces[0]]
        for k in range(1, n_z):
            pairs = [(z * n_y + y, (z + k) % n_z * n_y + y) for z in range(n_z) for y in range(n_y)]
            found.append(lax.ppermute(pieces[k], "sta", pairs))
        return found

    def over_z_at_once(pieces):
        groups = [[z * n_y + y for z in range(n_z)] for y in range(n_y)]
        return lax.all_to_all(pieces, "sta", 0, 0, axis_index_groups=groups, tiled=True)

    def over_y(cells):
        found = [cells]
        for k in range(1, n_y):
            pairs = [(z * n_y + y, z * n_y + (y + k) % n_y) for z in range(n_z) for y in range(n_y)]
            found.append(lax.ppermute(cells, "sta", pairs))
        return found

    def over_x(cells):
        found = [cells]
        for k in range(1, n_x):
            pairs = [(x * n_c + c, (x + k) % n_x * n_c + c) for x in range(n_x) for c in range(n_c)]
            found.append(lax.ppermute(cells, "day", pairs))
        return found

    def over_core(terms):
        pairs = [(j, j - j % n_c + (j + 1) % n_c) for j in range(n_day)]
        return terms[:1] + [lax.ppermute(term, "day", pairs) for term in terms[1:]]

    def over_all(*blocks):
        many = jnp.concatenate(blocks, axis=0) if len(blocks) > 1 else blocks[0]
        many = jnp.broadcast_to(many[None], (n_sta * n_day, *many.shape))
        return lax.all_to_all(many, ("sta", "day"), 0, 0, tiled=True)

    def back(value, k, size):
        return lax.rem(value + size - k, size)

    def space_row(place, i):
        return i * n_y + place[1]

    def space_col(shift):
        return lambda place, j: j * n_y + lax.rem(place[1] + n_y - shift, n_y)

    def time_row(place, i):
        return back(place[2], i, n_x) * n_c + place[3]

    def time_col(place, j):
        return place[2] * n_c + lax.rem(place[3] + j, n_c)

    def space_entries(shift, halves, earlier):
        col = space_col(shift)
        return entries_call(
            chain, coords, s_loc, n_z, n_z, space_row, col, space_range, STATIONS, "space_entries", halves, earlier
        )

    def space(cells, together):
        return space_call(chain, cells, matrices, together)

    def days(arrived):
        return over_core(time_call(chain, arrived, time, n_c))

    noise = noise[:, None]

    def sums(outer, p, hint=0):
        return sums_call(chain, observed, noise, residual, direction, outer, p, hint)

    def mask(p, together):
        return mask_call(chain, observed, direction, p, n_z, together)

    def pass_on(*groups, pieces=(), hint=0):
        found = gate_call(chain, [array for group in groups for array in group], pieces, hint)
        flat = iter(found)
        kept = [[next(flat) for _ in group] for group in groups]
        return kept + [found[-1]] if pieces else kept

    mask2 = mask(2, True)
    mask0 = mask(0, False)
    x2 = over_x(mask2)
    out0 = over_z(mask0)
    mask1 = mask(1, True)
    mask3 = mask(3, True)
    time = entries_call(chain, day_features, t_loc, n_x, n_c, time_row, time_col, time_range, DAYS, "time_entries")
    (mask1,), (mask3,), x2, cells0 = pass_on([mask1], [mask3], x2[1:], pieces=out0)

    out1 = over_z_at_once(mask1)
    x3 = over_x(mask3)
    y0 = over_y(cells0)
    terms2 = time_call(chain, [mask2] + x2, time, n_c)
    matrices = [space_entries(0, (0, 1), ())]
    x3, y0 = pass_on(x3[1:], y0[1:], hint=20 << 20)
    inner2 = add_call(chain, over_core(terms2), True)
    (cells1,), (inner2,) = pass_on([out1], [inner2])

    out2 = over_z_at_once(inner2)
    y1 = over_y(cells1)
    terms3 = time_call(chain, [mask3] + x3, time, n_c)
    for k in range(1, n_y):
        matrices.append(space_entries(k, (0, 1), ()))
    inner3 = add_call(chain, over_core(terms3), False)
    (cells2,), inner3 = pass_on([out2], inner3)

    out3 = over_z(inner3)
    y2 = over_y(cells2)
    smooth0 = space([cells0] + y0, False)
    smooth1 = space(y1, False)
    smooth0, smooth1, cells3 = pass_on(smooth0, smooth1, pieces=out3)

    home0 = over_z(smooth0)
    y3 = over_y(cells3)
    smooth2 = space(y2, False)
    smooth1, smooth2, home0 = pass_on(smooth1, smooth2, pieces=home0)

    home1 = over_z(smooth1)
    x0 = over_x(home0)
    smooth3 = space(y3, False)
    smooth2, smooth3, home1 = pass_on(smooth2, smooth3, pieces=home1)

    home2 = over_z(smooth2)
    x1 = over_x(home1)
    terms0 = time_call(chain, x0, time, n_c)
    home2, x1, terms0, smooth3 = pass_on(home2, x1[1:], terms0, smooth3)

    home3 = over_z(smooth3)
    outer0 = Outer(over_core(terms0))
    outer2 = Outer(home2)
    sums2 = sums(outer2, 2)
    sums0 = sums(outer0, 0)
    terms1 = time_call(chain, [home1] + x1, time, n_c)
    outer1 = Outer(over_core(terms1))
    outer3 = Outer(home3)
    sums3 = sums(outer3, 3, 200 << 20)
    sums1 = sums(outer1, 1)
    def update(stats, outers, first, earlier):
        given = (observed, noise, solution, residual, direction)
        return update_call(chain, stats, *given, outers, first, earlier)

    stats02 = over_all(sums0, sums2)
    stats13 = over_all(sums1, sums3)
    new = update(stats02, (outer0, outer2), 0, ())
    return tuple(update(stats13, (outer1, outer3), 1, new))


def solution(mesh):
    in_specs = (
        P(None, "sta", "day"),
        P(None, "sta", "day"),
        P(None, "sta", "day"),
        P("sta", "day"),
        P(),
        P(),
        P("sta"),
    )
    out_specs = (P(None, "sta", "day"), P(None, "sta", "day"), P(None, "sta", "day"))
    return jax.shard_map(shards, mesh=mesh, in_specs=in_specs, out_specs=out_specs, check_vma=False)
```

```python
import functools
import math

import jax
import jax.numpy as jnp
from jax import lax
from jax.experimental import pallas as pl
from jax.experimental.pallas import tpu as pltpu
from jax.sharding import PartitionSpec as P

STATIONS = 4096
DAYS = 4096
FEAT = 4

space_range = 0.5
time_range = 0.5

HBM = pltpu.MemorySpace.HBM
F32 = jnp.float32
BF16 = jnp.bfloat16


class Chain:
    def __init__(self, place):
        self.place = place
        self.token = None

    def __call__(self, body, name, grid, operands, in_specs, outs, out_specs, scratch=(), aliases=(), bytes_hint=0):
        operands, in_specs = list(operands), list(in_specs)
        n_in, n_tok = len(operands), 0 if self.token is None else 1
        if n_tok:
            operands.append(self.token)
            in_specs.append(pl.BlockSpec(memory_space=HBM))
        n_out = len(outs)

        def kernel(place, *refs):
            rest = refs[n_in + n_tok :]
            body(place, *refs[:n_in], *rest[:n_out], *rest[n_out + 1 :])

        found = pl.pallas_call(
            kernel,
            grid_spec=pltpu.PrefetchScalarGridSpec(
                num_scalar_prefetch=1,
                grid=grid,
                in_specs=in_specs,
                out_specs=list(out_specs) + [pl.BlockSpec(memory_space=HBM)],
                scratch_shapes=list(scratch),
            ),
            out_shape=[jax.ShapeDtypeStruct(*out) for out in outs] + [jax.ShapeDtypeStruct((8, 128), F32)],
            input_output_aliases={1 + k: v for k, v in aliases},
            compiler_params=pltpu.CompilerParams(vmem_limit_bytes=60 << 20),
            cost_estimate=pl.CostEstimate(flops=1150*bytes_hint, bytes_accessed=bytes_hint, transcendentals=0),
            name=name,
        )(self.place, *operands)
        self.token = found[-1]
        return list(found[:-1])


def rows_spec(*shape):
    lead = len(shape) - 2
    return pl.BlockSpec(shape, lambda i, place: (0,) * lead + (i, 0))


def columns_of(place, k, sign, parts, width):
    block = lax.rem(place[0] + (k if sign > 0 else parts - k), parts)
    return pl.ds(pl.multiple_of(block * width, width), width)


CHUNKS = 2


def mask_call(chain, observed, direction, probe, parts, together):
    _, s_loc, t_loc = direction.shape
    width, rows = t_loc // parts, s_loc // CHUNKS

    def body(place, seen, way, *out):
        for k in range(parts):
            if together:
                at = pl.ds(k * width, width)
                out[0][k] = seen[:, at].astype(F32) * way[0, :, at]
            else:
                at = columns_of(place, k, 1, parts, width)
                out[k][...] = seen[:, at].astype(F32) * way[0, :, at]

    if together:
        outs, specs = [((parts, s_loc, width), F32)], [rows_spec(parts, rows, width)]
    else:
        outs, specs = [((s_loc, width), F32)] * parts, [rows_spec(rows, width)] * parts
    found = chain(
        body,
        "mask",
        (CHUNKS,),
        (observed, direction),
        [
            rows_spec(rows, t_loc),
            pl.BlockSpec((1, rows, t_loc), lambda i, place: (probe, i, 0)),
        ],
        outs,
        specs,
    )
    return found[0] if together else found


def add_call(chain, terms, together):
    parts, s_loc, width = terms[0].shape
    rows = s_loc // CHUNKS

    def body(place, *refs):
        for k in range(parts):
            block = k if together else lax.rem(place[0] + k, parts)
            total = refs[0][block]
            for term in refs[1 : len(terms)]:
                total = total + term[block]
            if together:
                refs[len(terms)][k] = total
            else:
                refs[len(terms) + k][...] = total

    if together:
        outs, specs = [((parts, s_loc, width), F32)], [rows_spec(parts, rows, width)]
    else:
        outs, specs = [((s_loc, width), F32)] * parts, [rows_spec(rows, width)] * parts
    found = chain(body, "add", (CHUNKS,), terms, [rows_spec(parts, rows, width)] * len(terms), outs, specs)
    return found[0] if together else found


def gate_call(chain, arrays, pieces=(), hint=0):
    n, parts = len(arrays), len(pieces)
    anywhere = pl.BlockSpec(memory_space=pl.ANY)
    outs = [(array.shape, array.dtype) for array in arrays]

    def body(place, *refs):
        if parts:
            given, whole, (held, sems) = refs[n : n + parts], refs[2 * n + parts], refs[-2:]
            coming = [pltpu.make_async_copy(given[k], held.at[k], sems.at[k]) for k in range(parts)]
            for copy in coming:
                copy.start()
            going = []
            for k in range(parts):
                coming[k].wait()
                block = lax.rem(place[0] + parts - k, parts)
                going.append(pltpu.make_async_copy(held.at[k], whole.at[block], sems.at[parts + k]))
                going[k].start()
            for copy in going:
                copy.wait()

    if parts:
        outs.append(((parts, *pieces[0].shape), F32))
    return chain(
        body,
        "gate",
        (),
        [*arrays, *pieces],
        [anywhere] * (n + parts),
        outs,
        [anywhere] * len(outs),
        scratch=[pltpu.VMEM(outs[-1][0], F32), pltpu.SemaphoreType.DMA((2 * parts,))] if parts else (),
        aliases=[(k, k) for k in range(n)],
        bytes_hint=hint,
    )


def entries_call(chain, table, unit, n_rows, n_cols, row_block, col_block, reach, order, name, halves=(0, 1), earlier=()):
    features = table.shape[0]
    shape = (n_rows * unit, n_cols * unit)
    half, of = halves
    row_units = max(1, math.gcd(n_rows // of, 1024 // unit))
    col_units = max(1, math.gcd(n_cols, 1024 // unit))
    tile = (row_units * unit, col_units * unit)
    count = n_rows // of // row_units
    first = half * count
    shift = math.log(2.0 / order**0.5)
    step = 16

    def body(place, *refs):
        rows, cols = refs[:row_units], refs[row_units : row_units + col_units]
        high, low, across, down = refs[-4:]
        for u in range(col_units):
            for feature in range(features):
                line = cols[u][feature : feature + 1, :] * (1.0 / reach)
                across[feature, :, u * unit : (u + 1) * unit] = jnp.broadcast_to(line, (8, unit))
        for u in range(row_units):
            turned = jnp.concatenate([rows[u][...], jnp.zeros((8 - features, unit), F32)], axis=0).T * (1.0 / reach)
            for feature in range(features):
                down[feature, u * unit : (u + 1) * unit, :] = jnp.broadcast_to(turned[:, feature : feature + 1], (unit, 128))

        @pl.loop(0, tile[0] // step)
        def _(index):
            at = pl.ds(pl.multiple_of(index * step, step), step)
            total = None
            for feature in range(features):
                mine = jnp.concatenate([down[feature, at, :]] * (tile[1] // 128), axis=1)
                other = jnp.concatenate([across[feature]] * (step // 8), axis=0)
                diff = mine - other
                total = diff * diff if total is None else total + diff * diff
            dist = total * lax.rsqrt(jnp.maximum(total, 1e-37))
            high[at, :], low[at, :] = split(jnp.exp(shift - dist))

    def row_spec(u):
        return pl.BlockSpec((features, unit), lambda i, j, place: (0, row_block(place, (i + first) * row_units + u)))

    def col_spec(u):
        return pl.BlockSpec((features, unit), lambda i, j, place: (0, col_block(place, j * col_units + u)))

    out = pl.BlockSpec(tile, lambda i, j, place: (i + first, j))
    operands = [table] * (row_units + col_units)
    return chain(
        body,
        name,
        (count, n_cols // col_units),
        operands + list(earlier),
        [row_spec(u) for u in range(row_units)]
        + [col_spec(u) for u in range(col_units)]
        + [pl.BlockSpec(memory_space=HBM)] * len(earlier),
        [(shape, BF16)] * 2,
        [out, out],
        scratch=[pltpu.VMEM((features, 8, tile[1]), F32), pltpu.VMEM((features, tile[0], 128), F32)],
        aliases=[(len(operands) + k, k) for k in range(len(earlier))],
    )


def split(value):
    top = value.astype(BF16)
    return top, (value - top.astype(F32)).astype(BF16)


def dot(a, b):
    return jnp.dot(a, b, preferred_element_type=F32)


def space_call(chain, cells, matrices, together):
    parts, s_loc, width = cells[0].shape
    count = len(cells)
    span = parts * s_loc

    def body(place, *refs):
        mine, kern = refs[:count], refs[count : 3 * count]
        out, (cells_high, cells_low) = refs[3 * count : -2], refs[-2:]
        step = pl.program_id(0)

        @pl.when(step == 0)
        def _():
            for n in range(count):
                for b in range(parts):
                    at = pl.ds((n * parts + b) * s_loc, s_loc)
                    cells_high[at, :], cells_low[at, :] = split(mine[n][b])

        total = None
        for n in range(count):
            at = pl.ds(n * span, span)
            high, low = kern[2 * n], kern[2 * n + 1]
            term = dot(high[...], cells_high[at, :]) + dot(high[...], cells_low[at, :]) + dot(low[...], cells_high[at, :])
            total = term if total is None else total + term
        if together:
            out[0][0] = total
        else:
            for k in range(parts):

                @pl.when(step == k)
                def _():
                    out[k][...] = total

    whole = pl.BlockSpec((parts, s_loc, width), lambda i, place: (0, 0, 0))
    if together:
        matrix = pl.BlockSpec((s_loc, span), lambda i, place: (i, 0))
        outs, specs = [((parts, s_loc, width), F32)], [pl.BlockSpec((1, s_loc, width), lambda i, place: (i, 0, 0))]
    else:
        matrix = pl.BlockSpec((s_loc, span), lambda i, place: (lax.rem(place[0] + i, parts), 0))
        outs, specs = [((s_loc, width), F32)] * parts, [pl.BlockSpec((s_loc, width), lambda i, place: (0, 0))] * parts
    found = chain(
        body,
        "space",
        (parts,),
        list(cells) + [m for pair in matrices for m in pair],
        [whole] * count + [matrix] * (2 * count),
        outs,
        specs,
        scratch=[pltpu.VMEM((count * span, width), BF16)] * 2,
    )
    return found[0] if together else found


def time_call(chain, cells, matrix, cores):
    parts, s_loc, width = cells[0].shape
    count = len(cells)
    days = count * parts * width
    each = math.gcd(parts, 2)
    steps = parts // each

    def body(place, *refs):
        mine, (high, low) = refs[:count], refs[count : count + 2]
        out, (cells_high, cells_low) = refs[count + 2 : -2], refs[-2:]
        step = pl.program_id(0)

        @pl.when(step == 0)
        def _():
            for n in range(count):
                for b in range(parts):
                    at = pl.ds((n * parts + b) * width, width)
                    cells_high[:, at], cells_low[:, at] = split(mine[n][b])

        total = dot(cells_high[...], high[...]) + dot(cells_low[...], high[...]) + dot(cells_high[...], low[...])
        for c in range(cores):

            @pl.when(step // steps == c)
            def _():
                for e in range(each):
                    out[c][e] = total[:, e * width : (e + 1) * width]

    def out_spec(c):
        return pl.BlockSpec(
            (each, s_loc, width), lambda i, place: (jnp.clip(i - c * steps, 0, steps - 1), 0, 0)
        )

    whole = pl.BlockSpec((parts, s_loc, width), lambda i, place: (0, 0, 0))
    columns = pl.BlockSpec((days, each * width), lambda i, place: (0, i))
    return chain(
        body,
        "time",
        (steps * cores,),
        list(cells) + list(matrix),
        [whole] * count + [columns] * 2,
        [((parts, s_loc, width), F32)] * cores,
        [out_spec(c) for c in range(cores)],
        scratch=[pltpu.VMEM((s_loc, days), BF16)] * 2,
    )


class Outer:
    def __init__(self, refs):
        self.operands = list(refs)
        self.whole = refs[0].ndim == 3
        self.parts = refs[0].shape[0] if self.whole else len(refs)
        self.width = refs[0].shape[-1]

    def specs(self, rows):
        shape = (self.parts, rows, self.width) if self.whole else (rows, self.width)
        one = rows_spec(*shape)
        return [one] * len(self.operands)

    def each(self, place, refs):
        for k in range(self.parts):
            if self.whole:
                value = refs[0][k]
                for other in refs[1:]:
                    value = value + other[k]
                yield pl.ds(k * self.width, self.width), value
            else:
                yield columns_of(place, k, -1, self.parts, self.width), refs[k][...]


def sums_call(chain, observed, noise, residual, direction, outer, probe, bytes_hint=0):
    _, s_loc, t_loc = direction.shape
    rows = s_loc // CHUNKS
    n = len(outer.operands)

    def body(place, seen, var, res_ref, way_ref, *refs):
        out, total = refs[n:]
        step = pl.program_id(0)

        @pl.when(step == 0)
        def _():
            total[...] = jnp.zeros_like(total)

        for at, value in outer.each(place, refs[:n]):
            res, way = res_ref[0, :, at], way_ref[0, :, at]
            image = seen[:, at].astype(F32) * value + var[...] * way
            for row, product in enumerate((res * res, way * image, res * image, image * image)):
                total[row : row + 1, :] += jnp.sum(product, axis=0, keepdims=True)

        @pl.when(step == pl.num_programs(0) - 1)
        def _():
            out[...] = jnp.broadcast_to(jnp.sum(total[...], axis=1, keepdims=True), out.shape)

    probe_rows = pl.BlockSpec((1, rows, t_loc), lambda i, place: (probe, i, 0))
    return chain(
        body,
        "sums",
        (CHUNKS,),
        [observed, noise, residual, direction, *outer.operands],
        [rows_spec(rows, t_loc), rows_spec(rows, 1), probe_rows, probe_rows] + outer.specs(rows),
        [((8, 128), F32)],
        [pl.BlockSpec((8, 128), lambda i, place: (0, 0))],
        scratch=[pltpu.VMEM((8, outer.width), F32)],
        bytes_hint=bytes_hint,
    )[0]


def update_call(chain, stats, observed, noise, solution, residual, direction, outers, first, earlier):
    _, s_loc, t_loc = direction.shape
    rows = s_loc // CHUNKS

    def body(place, given, seen, var, sol_ref, res_ref, way_ref, *refs):
        new_solution, new_residual, new_direction = refs[-3:]
        taken = 0
        for p, outer in enumerate(outers):
            mine = refs[taken : taken + len(outer.operands)]
            taken += len(outer.operands)

            @pl.when(pl.program_id(0) // CHUNKS == p)
            def _():
                totals = jnp.sum(given[:, p * 8 : p * 8 + 8, :], axis=0)
                rr, pap, cross, square = (totals[k : k + 1, :1] for k in range(4))
                alpha = rr / pap
                rr_next = rr + alpha * (alpha * square - 2.0 * cross)
                beta = rr_next / rr
                for at, value in outer.each(place, mine):
                    way = way_ref[0, :, at]
                    image = seen[:, at].astype(F32) * value + var[...] * way
                    fresh = res_ref[0, :, at] - alpha * image
                    new_solution[0, :, at] = sol_ref[0, :, at] + alpha * way
                    new_residual[0, :, at] = fresh
                    new_direction[0, :, at] = fresh + beta * way

    def outer_specs(p, outer):
        def row(i):
            return jnp.clip(i - p * CHUNKS, 0, CHUNKS - 1)

        if outer.whole:
            one = pl.BlockSpec((outer.parts, rows, outer.width), lambda i, place: (0, row(i), 0))
        else:
            one = pl.BlockSpec((rows, outer.width), lambda i, place: (row(i), 0))
        return [one] * len(outer.operands)

    probe_rows = pl.BlockSpec((1, rows, t_loc), lambda i, place: (i // CHUNKS * 2 + first, i % CHUNKS, 0))
    operands = [stats, observed, noise, solution, residual, direction]
    operands += [ref for outer in outers for ref in outer.operands]
    return chain(
        body,
        "update",
        (len(outers) * CHUNKS,),
        operands + list(earlier),
        [
            pl.BlockSpec(stats.shape, lambda i, place: (0, 0, 0)),
            pl.BlockSpec((rows, t_loc), lambda i, place: (i % CHUNKS, 0)),
            pl.BlockSpec((rows, 1), lambda i, place: (i % CHUNKS, 0)),
            probe_rows,
            probe_rows,
            probe_rows,
        ]
        + [spec for p, outer in enumerate(outers) for spec in outer_specs(p, outer)]
        + [pl.BlockSpec(memory_space=HBM)] * len(earlier),
        [(direction.shape, F32)] * 3,
        [probe_rows] * 3,
        aliases=[(len(operands) + k, k) for k in range(len(earlier))],
    )


def shards(solution, residual, direction, observed, coords, day_features, noise):
    n_sta = lax.axis_size("sta")
    n_day = lax.axis_size("day")
    _, s_loc, t_loc = direction.shape
    n_z = math.gcd(n_sta, 4)
    n_y = n_sta // n_z
    n_c = math.gcd(n_day, 2)
    n_x = n_day // n_c
    sta = lax.axis_index("sta")
    day = lax.axis_index("day")
    place = jnp.stack([sta // n_y, sta % n_y, day // n_c, day % n_c]).astype(jnp.int32)
    chain = Chain(place)

    def over_z(pieces):
        found = [pieces[0]]
        for k in range(1, n_z):
            pairs = [(z * n_y + y, (z + k) % n_z * n_y + y) for z in range(n_z) for y in range(n_y)]
            found.append(lax.ppermute(pieces[k], "sta", pairs))
        return found

    def over_z_at_once(pieces):
        groups = [[z * n_y + y for z in range(n_z)] for y in range(n_y)]
        return lax.all_to_all(pieces, "sta", 0, 0, axis_index_groups=groups, tiled=True)

    def over_y(cells):
        found = [cells]
        for k in range(1, n_y):
            pairs = [(z * n_y + y, z * n_y + (y + k) % n_y) for z in range(n_z) for y in range(n_y)]
            found.append(lax.ppermute(cells, "sta", pairs))
        return found

    def over_x(cells):
        found = [cells]
        for k in range(1, n_x):
            pairs = [(x * n_c + c, (x + k) % n_x * n_c + c) for x in range(n_x) for c in range(n_c)]
            found.append(lax.ppermute(cells, "day", pairs))
        return found

    def over_core(terms):
        pairs = [(j, j - j % n_c + (j + 1) % n_c) for j in range(n_day)]
        return terms[:1] + [lax.ppermute(term, "day", pairs) for term in terms[1:]]

    def over_all(*blocks):
        many = jnp.concatenate(blocks, axis=0) if len(blocks) > 1 else blocks[0]
        many = jnp.broadcast_to(many[None], (n_sta * n_day, *many.shape))
        return lax.all_to_all(many, ("sta", "day"), 0, 0, tiled=True)

    def back(value, k, size):
        return lax.rem(value + size - k, size)

    def space_row(place, i):
        return i * n_y + place[1]

    def space_col(shift):
        return lambda place, j: j * n_y + lax.rem(place[1] + n_y - shift, n_y)

    def time_row(place, i):
        return back(place[2], i, n_x) * n_c + place[3]

    def time_col(place, j):
        return place[2] * n_c + lax.rem(place[3] + j, n_c)

    def space_entries(shift, halves, earlier):
        col = space_col(shift)
        return entries_call(
            chain, coords, s_loc, n_z, n_z, space_row, col, space_range, STATIONS, "space_entries", halves, earlier
        )

    def space(cells, together):
        return space_call(chain, cells, matrices, together)

    def days(arrived):
        return over_core(time_call(chain, arrived, time, n_c))

    noise = noise[:, None]

    def sums(outer, p, hint=0):
        return sums_call(chain, observed, noise, residual, direction, outer, p, hint)

    def mask(p, together):
        return mask_call(chain, observed, direction, p, n_z, together)

    def pass_on(*groups, pieces=(), hint=0):
        found = gate_call(chain, [array for group in groups for array in group], pieces, hint)
        flat = iter(found)
        kept = [[next(flat) for _ in group] for group in groups]
        return kept + [found[-1]] if pieces else kept

    mask2 = mask(2, True)
    mask0 = mask(0, False)
    x2 = over_x(mask2)
    out0 = over_z(mask0)
    mask1 = mask(1, True)
    mask3 = mask(3, True)
    time = entries_call(chain, day_features, t_loc, n_x, n_c, time_row, time_col, time_range, DAYS, "time_entries")
    (mask1,), (mask3,), x2, cells0 = pass_on([mask1], [mask3], x2[1:], pieces=out0)

    out1 = over_z_at_once(mask1)
    x3 = over_x(mask3)
    y0 = over_y(cells0)
    terms2 = time_call(chain, [mask2] + x2, time, n_c)
    matrices = [space_entries(0, (0, 1), ())]
    x3, y0 = pass_on(x3[1:], y0[1:], hint=20 << 20)
    inner2 = add_call(chain, over_core(terms2), True)
    (cells1,), (inner2,) = pass_on([out1], [inner2])

    out2 = over_z_at_once(inner2)
    y1 = over_y(cells1)
    terms3 = time_call(chain, [mask3] + x3, time, n_c)
    for k in range(1, n_y):
        matrices.append(space_entries(k, (0, 1), ()))
    inner3 = add_call(chain, over_core(terms3), False)
    (cells2,), inner3 = pass_on([out2], inner3)

    out3 = over_z(inner3)
    y2 = over_y(cells2)
    smooth0 = space([cells0] + y0, False)
    smooth1 = space(y1, False)
    smooth0, smooth1, cells3 = pass_on(smooth0, smooth1, pieces=out3)

    home0 = over_z(smooth0)
    y3 = over_y(cells3)
    smooth2 = space(y2, False)
    smooth1, smooth2, home0 = pass_on(smooth1, smooth2, pieces=home0)

    home1 = over_z(smooth1)
    x0 = over_x(home0)
    smooth3 = space(y3, False)
    smooth2, smooth3, home1 = pass_on(smooth2, smooth3, pieces=home1)

    home2 = over_z(smooth2)
    x1 = over_x(home1)
    terms0 = time_call(chain, x0, time, n_c)
    home2, terms0, smooth3 = pass_on(home2, terms0, smooth3)

    home3 = over_z(smooth3)
    outer0 = Outer(over_core(terms0))
    outer2 = Outer(home2)
    sums2 = sums(outer2, 2)
    (x1,) = pass_on(x1[1:], hint=20 << 20)
    sums0 = sums(outer0, 0)
    terms1 = time_call(chain, [home1] + x1, time, n_c)
    outer1 = Outer(over_core(terms1))
    outer3 = Outer(home3)
    sums3 = sums(outer3, 3, 200 << 20)
    sums1 = sums(outer1, 1)
    def update(stats, outers, first, earlier):
        given = (observed, noise, solution, residual, direction)
        return update_call(chain, stats, *given, outers, first, earlier)

    stats02 = over_all(sums0, sums2)
    stats13 = over_all(sums1, sums3)
    new = update(stats02, (outer0, outer2), 0, ())
    return tuple(update(stats13, (outer1, outer3), 1, new))


def solution(mesh):
    in_specs = (
        P(None, "sta", "day"),
        P(None, "sta", "day"),
        P(None, "sta", "day"),
        P("sta", "day"),
        P(),
        P(),
        P("sta"),
    )
    out_specs = (P(None, "sta", "day"), P(None, "sta", "day"), P(None, "sta", "day"))
    return jax.shard_map(shards, mesh=mesh, in_specs=in_specs, out_specs=out_specs, check_vma=False)
```
